128 devices in a mesh: gx: 32 (over x, z, core), gz: 4 (over y).
Axes of the slice: x: 4, y: 4, z: 4, core: 2. Of those that a mesh axis runs over, the one named last changes fastest.
Arguments:
- vorticity: float32 [3, 128, 16384], P(None, None, ('gx', 'gz')), may hold values from -6 to 6
- position: float32 [3, 128, 16384], P(None, None, ('gx', 'gz')), may hold values from 1 to 6, as said below
- counts: int32 [4, 16384], P(None, ('gx', 'gz')), may hold values from 0 to 32
- owner_ids: int32 [32768, 1], P(('gx', 'gz')), may hold values from 0 to 127; in each aligned block of 256 rows (0 to 255, 256 to 511, ...) at most 4 rows name the same one
- slot_ids: int32 [32768], P(('gx', 'gz')), may hold values from 0 to 1023
- velocity: float32 [128, 16, 64, 3, 128], P('gx', None, 'gz'), may hold values from -6 to 6
Outputs:
- mesh_vorticity: float32 [128, 16, 64, 3, 128], P('gx', None, 'gz')
- stretching: float32 [2, 3, 128, 16384], P(None, None, None, ('gx', 'gz'))
The draws below stay inside these ranges and needn't reach their ends.
Inputs may be any that keep to these rules, and one draw needn't show every extreme that they name: `owner_ids`: among the routed tiles of one domain no owner is named more than 4 times, a bound that some block reaches. `position`: coordinates 0 and 1 lie in [1, 2), coordinate 2 in [1, 6).
All inputs are finite; a program needn't handle non-finite values.
Results may differ from the reference program's by a relative error of at most 0.0003.
Values sent between devices are 32-bit elements; how exact they have to be, the bound alone decides.
No kernel may reach another device: no remote copies, remote signals or barrier semaphores. Data moves between devices by JAX's collectives and lax.ppermute only.
A program may use at most 256 MiB of HBM per device.

```python
import math
import jax
import jax.numpy as jnp
import numpy as np
from jax import lax

CELLS_X = 16
CELLS_Y = 64
CELLS_Z = 128
TILES_DEV = 128
PARTICLES = 128
PATCH = 128
QUARTER = 32
CAPACITY = 4
TILES = 16384
ROUTED = 32768
SLOT_COUNT = 1024
SLOTS_X = 128
SLOTS_Y = 16
SLOTS_Z = 64
N_GX = 32
N_GZ = 4
DEVICES = 128


def draw_position(key, part):
    unit = jax.random.uniform(key, (3, PARTICLES, TILES), jnp.float32)
    reach = jnp.array([1.0, 1.0, 5.0], jnp.float32)
    return 1.0 + unit * reach[:, None, None]


def place_ends(result, key, smallest, largest):
    index_at = [jax.random.randint(jax.random.fold_in(key, axis), (), 0, length) for axis, length in enumerate(result.shape)]
    widest = result.shape.index(max(result.shape))
    neighbour = index_at[:widest] + [(index_at[widest] + 1) % result.shape[widest]] + index_at[widest + 1:]
    return result.at[tuple(index_at)].set(smallest).at[tuple(neighbour)].set(largest)


def block_scale(key, dims, pieces, smallest, largest):
    factor_of = 1.0
    for dim, parts in pieces:
        draws = jax.random.uniform(jax.random.fold_in(jax.random.fold_in(key, 6), dim), (parts,), jnp.float32, smallest / len(pieces), largest / len(pieces))
        factor_of = factor_of * jnp.repeat(jnp.exp(draws), dims[dim] // parts).reshape((-1,) + (1,) * (len(dims) - 1 - dim))
    return factor_of


def routed_block(rng, own, number, rows, amount, top, bound, slope):
    order = jax.random.permutation(rng, amount)
    heavy_load, ordinary = load_shares(amount, rows * top, bound, slope, True), load_shares(amount, rows * top, bound, slope, False)
    places = jnp.arange(amount)

    def named(tallies, offset_by):
        used = int((tallies > 0).sum())
        fixed = max(1, used // 4)
        shifted = fixed + (places - fixed + offset_by * (used - fixed)) % max(1, amount - fixed)
        return jnp.zeros((amount,), jnp.int32).at[order[jnp.where(places < fixed, places, shifted)]].set(jnp.asarray(tallies, jnp.int32))

    tallies = jnp.where(number % 4 == 0, named(heavy_load, number // 4), named(ordinary, number - number // 4 - 1))
    mixed = jax.random.permutation(jax.random.fold_in(own, 3), amount)
    giver, taker = mixed[0:amount // 2 * 2:2], mixed[1:amount // 2 * 2:2]
    room = jnp.minimum(tallies[giver] - 1, bound - tallies[taker]) // 2
    room = jnp.where((giver == order[0]) | (taker == order[0]) | (tallies[taker] == 0), 0, jnp.maximum(room, 0))
    shifted = jax.random.randint(jax.random.fold_in(own, 4), (amount // 2,), 0, 1 << 20) % (room + 1)
    tallies = tallies.at[giver].add(-shifted).at[taker].add(shifted)
    members = jnp.searchsorted(jnp.cumsum(tallies), jnp.arange(rows * top), side="right").astype(jnp.int32)
    table = members.reshape(top, rows).T
    table = table[jax.random.permutation(jax.random.fold_in(own, 1), rows)]
    offset_by = jax.random.randint(jax.random.fold_in(own, 2), (rows, 1), 0, top)
    return jnp.take_along_axis(table, (jnp.arange(top)[None, :] + offset_by) % top, axis=1)


def load_shares(amount, total, bound, skew, full):
    loads = [(1 << 20) // math.isqrt(grade ** skew) + 1 for grade in range(1, amount + 1)]
    largest = bound if full else min(bound, max(-(-total // amount), total * loads[0] // sum(loads)))
    least = 1 if total - largest >= amount - 1 else 0
    given, surplus = [largest] + [least] * (amount - 1), total - largest - least * (amount - 1)
    while surplus > 0:
        movable = [i for i in range(1, amount) if given[i] < largest] or [i for i in range(1, amount) if given[i] < bound]
        pool, budget = sum([loads[i] for i in movable]), surplus
        for i in movable:
            extra = min(bound - given[i], max(1, budget * loads[i] // pool), surplus)
            given[i] = given[i] + extra
            surplus = surplus - extra
    return np.array(given)


def centred(key, shape, deviation, limit, pieces=(), kind=jnp.bfloat16):
    loudness = block_scale(key, shape, pieces, -0.22, 0.18) if pieces else 1.0
    entries = jax.random.normal(key, shape, jnp.float32) * deviation * loudness
    return jnp.minimum(jnp.maximum(entries, -limit), limit).astype(kind)


def setup_inputs(seed: int = 0) -> dict:
    splits = jax.random.split(jax.random.key(seed), 7)
    vorticity = centred(splits[0], (3, PARTICLES, TILES), 1.0, 6.0, ((2, 128),), jnp.float32)
    position = draw_position(jax.random.fold_in(splits[6], 71), 0)
    counts = place_ends(jax.random.randint(splits[2], (4, TILES), 0, QUARTER + 1), jax.random.fold_in(splits[2], 1), 0, QUARTER).astype(jnp.int32)
    owner_ids_keys = jax.random.split(jax.random.fold_in(splits[3], 1), ROUTED // (2 * TILES_DEV))
    owner_ids_turns = jax.random.permutation(jax.random.fold_in(splits[3], 3), ROUTED // (2 * TILES_DEV))
    owner_ids = jax.vmap(lambda own, number: routed_block(jax.random.fold_in(splits[3], 2), own, number, 2 * TILES_DEV, DEVICES, 1, CAPACITY, 2))(owner_ids_keys, owner_ids_turns).reshape((ROUTED, 1))
    slot_ids = place_ends(jax.random.randint(splits[4], (ROUTED,), 0, SLOT_COUNT), jax.random.fold_in(splits[4], 1), 0, SLOT_COUNT - 1).astype(jnp.int32)
    velocity = centred(splits[5], (SLOTS_X, SLOTS_Y, SLOTS_Z, 3, PATCH), 1.0, 6.0, ((0, 32), (2, 4)), jnp.float32)
    return dict(vorticity=vorticity, position=position, counts=counts, owner_ids=owner_ids, slot_ids=slot_ids, velocity=velocity)


def m4prime(offset):
    radius = jnp.abs(offset)
    inner_part = 1.0 - 2.5 * radius * radius + 1.5 * radius * radius * radius
    outer_part = 0.5 * (2.0 - radius) * (2.0 - radius) * (1.0 - radius)
    return jnp.where(radius < 1.0, inner_part, jnp.where(radius < 2.0, outer_part, jnp.zeros_like(radius)))


def kernel_table(coords):
    float_type = coords.dtype
    cells = jnp.arange(128, dtype=jnp.int32)
    cell_x = (cells // 32).astype(float_type)
    cell_y = ((cells // 8) % 4).astype(float_type)
    cell_z = (cells % 8).astype(float_type)
    return (m4prime(cell_x[None, None, :] - coords[:, 0, :, None])
            * m4prime(cell_y[None, None, :] - coords[:, 1, :, None])
            * m4prime(cell_z[None, None, :] - coords[:, 2, :, None]))


def cell_offset(center, after, before, stride, per, offset):
    lanes = jnp.arange(128, dtype=jnp.int32)
    digit = (lanes // stride) % per + offset
    same = jnp.roll(center, -offset * stride, axis=-1)
    ahead = jnp.roll(after, -(offset - per) * stride, axis=-1)
    behind = jnp.roll(before, -(offset + per) * stride, axis=-1)
    return jnp.where(digit >= per, ahead, jnp.where(digit < 0, behind, same))


def sixth_order(getter):
    return (45.0 * (getter(1) - getter(-1)) - 9.0 * (getter(2) - getter(-2)) + (getter(3) - getter(-3))) / 60.0


def velocity_gradient(padded):
    field_x = padded[:, :, 1:-1]
    field_z = padded[1:-1]
    inner = padded[1:-1, :, 1:-1]
    after_y = jnp.roll(inner, -1, axis=1)
    before_y = jnp.roll(inner, 1, axis=1)
    along_x = sixth_order(lambda offset: cell_offset(field_x[1:-1], field_x[2:], field_x[:-2], 32, 4, offset))
    along_y = sixth_order(lambda offset: cell_offset(inner, after_y, before_y, 8, 4, offset))
    along_z = sixth_order(lambda offset: cell_offset(field_z[:, :, 1:-1], field_z[:, :, 2:], field_z[:, :, :-2], 1, 8, offset))
    stacked = jnp.stack([along_x, along_y, along_z], axis=4)
    return stacked.reshape(stacked.shape[:3] + (9, 128))


def sample_rows(grads, vortex, coords):
    sampled = jnp.einsum("bkc,bpc->bkp", grads, kernel_table(coords), precision=lax.Precision.HIGHEST)
    sampled = sampled.reshape(sampled.shape[0], 3, 3, sampled.shape[2])
    return jnp.sum(sampled * vortex[:, None, :, :], axis=2)


def from_neighbour(operand, axis, forward):
    extent = operand.shape[axis]
    hollow = jnp.zeros_like(lax.slice_in_dim(operand, 0, 1, axis=axis))
    if forward:
        return jnp.concatenate([hollow, lax.slice_in_dim(operand, 0, extent - 1, axis=axis)], axis=axis)
    return jnp.concatenate([lax.slice_in_dim(operand, 1, extent, axis=axis), hollow], axis=axis)


def reference(vorticity, position, counts, owner_ids, slot_ids, velocity):
    quarter = PARTICLES // 4
    domains = N_GX * N_GZ
    vortex = vorticity.reshape(3, PARTICLES, N_GX, N_GZ, TILES_DEV)
    coords = position.reshape(3, PARTICLES, N_GX, N_GZ, TILES_DEV)
    moves = counts.reshape(4, N_GX, N_GZ, TILES_DEV)
    lane_ids = jnp.arange(quarter, dtype=jnp.int32)
    leave_masks = []
    arrived_vortex = []
    arrived_coords = []
    for heading in range(4):
        mask_now = (lane_ids[:, None, None, None] < moves[heading][None]).astype(vorticity.dtype)
        leave_masks.append(mask_now)
        part_vortex = vortex[:, heading * quarter:(heading + 1) * quarter] * mask_now
        part_coords = coords[:, heading * quarter:(heading + 1) * quarter] * mask_now
        axis_now = 2 if heading < 2 else 3
        forward = heading % 2 == 0
        arrived_vortex.append(from_neighbour(part_vortex, axis_now, forward))
        arrived_coords.append(from_neighbour(part_coords, axis_now, forward))
    leaving = jnp.concatenate(leave_masks, axis=0)
    kept_vortex = vortex * (1.0 - leaving)[None]
    routed_vortex = jnp.concatenate([kept_vortex, jnp.concatenate(arrived_vortex, axis=1)], axis=4)
    routed_coords = jnp.concatenate([coords, jnp.concatenate(arrived_coords, axis=1)], axis=4)
    routed_vortex = jnp.transpose(routed_vortex, (2, 3, 4, 0, 1)).reshape(domains, 2 * TILES_DEV, 3, PARTICLES)
    routed_coords = jnp.transpose(routed_coords, (2, 3, 4, 0, 1)).reshape(domains, 2 * TILES_DEV, 3, PARTICLES)

    def deposit_block(operands):
        block_vortex, block_coords = operands
        return jnp.einsum("bip,bpc->bic", block_vortex, kernel_table(block_coords), precision=lax.Precision.HIGHEST)

    patches = lax.map(deposit_block, (routed_vortex, routed_coords)).reshape(ROUTED, 3, 128)
    owners = owner_ids[:, 0]
    targets = owners * SLOT_COUNT + slot_ids
    summed = jax.ops.segment_sum(patches, targets, num_segments=domains * SLOT_COUNT)
    slots_x = CELLS_X // 4
    slots_y = CELLS_Y // 4
    slots_z = CELLS_Z // 8
    blocks = summed.reshape(N_GX, N_GZ, slots_x, slots_y, slots_z, 3, 128)
    mesh_vorticity = jnp.transpose(blocks, (0, 2, 3, 1, 4, 5, 6)).reshape(SLOTS_X, SLOTS_Y, SLOTS_Z, 3, 128)

    padded = jnp.pad(velocity, ((1, 1), (0, 0), (1, 1), (0, 0), (0, 0)))
    gradient = velocity_gradient(padded)

    def sample_block(operands):
        block_owner, block_slot, block_vortex, block_coords = operands
        index_x = ((block_owner // N_GZ) * slots_x + block_slot // (slots_y * slots_z)).astype(jnp.int32)
        index_y = ((block_slot // slots_z) % slots_y).astype(jnp.int32)
        index_z = ((block_owner % N_GZ) * slots_z + block_slot % slots_z).astype(jnp.int32)
        grads = gradient[index_x, index_y, index_z]
        return sample_rows(grads, block_vortex, block_coords)

    stretch_rows = lax.map(sample_block, (owners.reshape(domains, 2 * TILES_DEV), slot_ids.reshape(domains, 2 * TILES_DEV), routed_vortex, routed_coords))
    stretch_rows = stretch_rows.reshape(N_GX, N_GZ, 2, TILES_DEV, 3, PARTICLES)
    stretching = jnp.transpose(stretch_rows, (2, 4, 5, 0, 1, 3)).reshape(2, 3, PARTICLES, TILES)
    return mesh_vorticity, stretching
```

```python
import jax
import jax.numpy as jnp
from jax import lax
from jax.experimental import pallas as pl
from jax.experimental.pallas import tpu as pltpu
from jax.sharding import PartitionSpec as P

AXES = ("gx", "gz")
F32 = jnp.float32
BF16 = jnp.bfloat16
VMEM = pl.BlockSpec(memory_space=pltpu.VMEM)
SMEM = pl.BlockSpec(memory_space=pltpu.SMEM)
PARAMS = pltpu.CompilerParams(vmem_limit_bytes=40 * 1024 * 1024)
GRAD_ROWS = 64 * 9 * 16
GRAD_PAD = 128


def sds(shape, dtype=F32):
    return jax.ShapeDtypeStruct(shape, dtype)


def cost(flops, read):
    return pl.CostEstimate(flops=flops, bytes_accessed=read, transcendentals=0)


def depart_kernel(vort, pos, counts, *outs):
    place = lax.broadcasted_iota(jnp.int32, (32, 128), 0)
    for heading in range(4):
        leaves = place < counts[heading : heading + 1, :]
        rows = slice(heading * 32, heading * 32 + 32)
        for i in range(3):
            outs[heading][i] = jnp.where(leaves, vort[i, rows, :], 0.0)
            outs[heading][3 + i] = jnp.where(leaves, pos[i, rows, :], 0.0)


def depart(vort, pos, counts):
    return pl.pallas_call(
        depart_kernel,
        out_shape=[sds((6, 32, 128))] * 4,
        in_specs=[VMEM] * 3,
        out_specs=[VMEM] * 4,
        compiler_params=PARAMS,
        cost_estimate=cost(400_000, 1_600_000),
    )(vort, pos, counts)


def plan_kernel(owners, slots, places, marks, tally):
    def clear(i, carry):
        tally[i] = 0
        for k in range(4):
            marks[4 * i + k] = 0
        return carry

    lax.fori_loop(0, 128, clear, 0)

    def step(r, carry):
        owner = owners[r]
        rank = tally[owner]
        tally[owner] = rank + 1
        places[r] = owner * 4 + rank
        marks[owner * 4 + rank] = slots[r]
        return carry

    lax.fori_loop(0, 256, step, 0, unroll=4)


def plan(owners, slots):
    return pl.pallas_call(
        plan_kernel,
        out_shape=[sds((256,), jnp.int32), sds((512,), jnp.int32)],
        in_specs=[SMEM] * 2,
        out_specs=[SMEM] * 2,
        scratch_shapes=[pltpu.SMEM((128,), jnp.int32)],
        cost_estimate=cost(4_000, 6_000),
    )(owners, slots)


ORDER = (3, 4, 0, 1, 2, 5)


def route_kernel(places, vort, pos, counts, a0, a1, a2, a3, ship, turned):
    arrivals = (a0, a1, a2, a3)

    def clear(i, carry):
        ship[pl.ds(pl.multiple_of(i * 64, 64), 64), :] = jnp.zeros((64, 128), F32)
        return carry

    lax.fori_loop(0, 48, clear, 0)
    place = lax.broadcasted_iota(jnp.int32, (32, 128), 0)
    leaves = [place < counts[heading : heading + 1, :] for heading in range(4)]
    for at, comp in enumerate(ORDER):
        if comp < 3:
            kept = jnp.concatenate(
                [
                    jnp.where(leaves[h], 0.0, vort[comp, 32 * h : 32 * h + 32, :])
                    for h in range(4)
                ],
                axis=0,
            )
        else:
            kept = pos[comp - 3]
        turned[at * 256 : at * 256 + 128, :] = kept.T
        came = jnp.concatenate([a[comp] for a in arrivals], axis=0)
        turned[at * 256 + 128 : at * 256 + 256, :] = came.T

    def move(r, carry):
        place = places[r]
        base = (place >> 2) * 24 + (place & 3)
        ship[pl.ds(base, 6, stride=4), :] = turned[pl.ds(r, 6, stride=256), :]
        return carry

    lax.fori_loop(0, 256, move, 0, unroll=8)


def route(places, vort, pos, counts, arrivals):
    return pl.pallas_call(
        route_kernel,
        out_shape=sds((3072, 128)),
        in_specs=[SMEM] + [VMEM] * 7,
        out_specs=VMEM,
        scratch_shapes=[pltpu.VMEM((1536, 128), F32)],
        compiler_params=PARAMS,
        cost_estimate=cost(1_000_000, 4_000_000),
    )(places, vort, pos, counts, *arrivals)


def gradient_kernel(vel, xb, xa, zb, za, out):
    lane = lax.broadcasted_iota(jnp.int32, (16, 128), 1)
    digit_y = (lane // 8) % 4
    digit_z = lane % 8

    def shift(value, by):
        return pltpu.roll(value, by % 128, 1)

    def derive(sx, sy, i):
        c = vel[sx, sy, i]
        before = vel[sx - 1, sy, i] if sx > 0 else xb[sy, i]
        after = vel[sx + 1, sy, i] if sx < 3 else xa[sy, i]
        plus = [shift(jnp.where(lane < 32 * o, after, c), -32 * o) for o in (1, 2, 3)]
        minus = [shift(jnp.where(lane >= 128 - 32 * o, before, c), 32 * o) for o in (1, 2, 3)]
        along_x = combine(plus, minus)

        before = vel[sx, (sy + 15) & 15, i]
        after = vel[sx, (sy + 1) & 15, i]
        plus = [
            jnp.where(digit_y >= 4 - o, shift(after, 32 - 8 * o), shift(c, -8 * o))
            for o in (1, 2, 3)
        ]
        minus = [
            jnp.where(digit_y < o, shift(before, 8 * o - 32), shift(c, 8 * o)) for o in (1, 2, 3)
        ]
        along_y = combine(plus, minus)

        before = jnp.concatenate([zb[sx, sy, i], c[:15]], axis=0)
        after = jnp.concatenate([c[1:], za[sx, sy, i]], axis=0)
        plus = [
            jnp.where(digit_z >= 8 - o, shift(after, 8 - o), shift(c, -o)) for o in (1, 2, 3)
        ]
        minus = [jnp.where(digit_z < o, shift(before, o - 8), shift(c, o)) for o in (1, 2, 3)]
        along_z = combine(plus, minus)
        return along_x, along_y, along_z

    def combine(plus, minus):
        return (
            (45.0 / 60.0) * (plus[0] - minus[0])
            - (9.0 / 60.0) * (plus[1] - minus[1])
            + (1.0 / 60.0) * (plus[2] - minus[2])
        )

    for sx in range(4):

        def per_y(sy, carry, sx=sx):
            base = (sx * 16 + sy) * 144
            for i in range(3):
                for j, value in enumerate(derive(sx, sy, i)):
                    row = pl.multiple_of(base + (j * 3 + i) * 16, 16)
                    out[pl.ds(row, 16), :] = value
            return carry

        lax.fori_loop(0, 16, per_y, 0)
    out[GRAD_ROWS:, :] = jnp.zeros((GRAD_PAD, 128), F32)


def gradient(vel, xb, xa, zb, za):
    return pl.pallas_call(
        gradient_kernel,
        out_shape=sds((GRAD_ROWS + GRAD_PAD, 128)),
        in_specs=[VMEM] * 5,
        out_specs=VMEM,
        compiler_params=PARAMS,
        cost_estimate=cost(20_000_000, 8_000_000),
    )(vel, xb, xa, zb, za)


def split(value):
    high = value.astype(BF16)
    return high, (value - high.astype(F32)).astype(BF16)


def owner_kernel(marks, rows, grads, mesh, back):
    def clear(i, carry):
        mesh[pl.ds(pl.multiple_of(i * 64, 64), 64), :] = jnp.zeros((64, 128), F32)
        return carry

    lax.fori_loop(0, 48, clear, 0)
    cell_z = lax.broadcasted_iota(jnp.int32, (8, 128), 0).astype(F32)

    def wide(row):
        return jnp.broadcast_to(row, (8, 128))

    def per_source(s, carry):
        base = pl.multiple_of(s * 24, 8)
        f = rows[pl.ds(base, 8), :] - 1.0
        g = 1.0 - f
        weights = (
            -0.5 * f * g * g,
            1.0 + f * f * (1.5 * f - 2.5),
            1.0 + g * g * (1.5 * g - 2.5),
            -0.5 * g * f * f,
        )
        for k in range(4):
            slot = marks[s * 4 + k]
            column = slot >> 4
            level = slot & 15
            z = wide(rows[pl.ds(base + 20 + k, 1), :])
            radius = jnp.abs(cell_z - z)
            rest = jnp.maximum(2.0 - radius, 0.0)
            along_z = jnp.where(
                radius < 1.0,
                1.0 + radius * radius * (1.5 * radius - 2.5),
                0.5 * rest * rest * (1.0 - radius),
            )
            yz = [wide(weights[b][4 + k : 5 + k]) * along_z for b in range(4)]
            xs = [wide(weights[a][k : k + 1]) for a in range(4)]
            table = jnp.concatenate([xs[a] * yz[b] for a in range(4) for b in range(4)], axis=0)
            high, low = split(table)

            vortex = [rows[pl.ds(base + 8 + 4 * j + k, 1), :] for j in range(3)]
            grad = jnp.concatenate(
                [
                    grads[pl.ds(column * 144 + j * 48 + level, 8, stride=16), :]
                    for j in range(3)
                ],
                axis=0,
            )
            g_high, g_low = split(grad)
            left = jnp.concatenate([g_high, g_low], axis=0)
            left = jnp.concatenate([left, left], axis=1)
            sampled = jnp.dot(
                left, jnp.concatenate([high, low], axis=0), preferred_element_type=F32
            )
            sampled = sampled[:24] + sampled[24:]
            stretch = (
                sampled[0:8] * wide(vortex[0])
                + sampled[8:16] * wide(vortex[1])
                + sampled[16:24] * wide(vortex[2])
            )
            back[pl.ds(s * 12 + k, 3, stride=4), :] = stretch[:3]

            v = rows[pl.ds(base + 8 + k, 3, stride=4), :]
            v = jnp.concatenate([v, jnp.zeros((5, 128), F32)], axis=0)
            v_high, v_low = split(v)
            left = jnp.concatenate([v_high, v_low], axis=0)
            left = jnp.concatenate([left, left], axis=1)
            patch = lax.dot_general(
                left,
                jnp.concatenate([high, low], axis=1),
                (((1,), (1,)), ((), ())),
                preferred_element_type=F32,
            )
            patch = patch[:3] + patch[8:11]
            at = pl.ds(column * 48 + level, 3, stride=16)
            mesh[at, :] = mesh[at, :] + patch
        return carry

    lax.fori_loop(0, 128, per_source, 0)


def owner_work(marks, rows, grads):
    return pl.pallas_call(
        owner_kernel,
        out_shape=[sds((3072, 128)), sds((1536, 128))],
        in_specs=[SMEM, VMEM, VMEM],
        out_specs=[VMEM] * 2,
        compiler_params=PARAMS,
        cost_estimate=cost(300_000_000, 9_000_000),
    )(marks, rows, grads)


def unpack_kernel(places, back, out, turned):
    def move(r, carry):
        place = places[r]
        base = (place >> 2) * 12 + (place & 3)
        turned[pl.ds(r, 3, stride=256), :] = back[pl.ds(base, 3, stride=4), :]
        return carry

    lax.fori_loop(0, 256, move, 0, unroll=8)
    for h in range(2):
        for i in range(3):
            at = i * 256 + h * 128
            out[h, i] = turned[at : at + 128, :].T


def unpack(places, back):
    return pl.pallas_call(
        unpack_kernel,
        out_shape=sds((2, 3, 128, 128)),
        in_specs=[SMEM, VMEM],
        out_specs=VMEM,
        scratch_shapes=[pltpu.VMEM((768, 128), F32)],
        compiler_params=PARAMS,
        cost_estimate=cost(1_000_000, 2_000_000),
    )(places, back)


def stepped(value, axis, step):
    count = lax.axis_size(axis)
    first, last = (max(0, -step), min(count, count - step))
    return lax.ppermute(value, axis, [(source, source + step) for source in range(first, last)])


def exchange(value):
    return lax.all_to_all(value, AXES, split_axis=0, concat_axis=0, tiled=True)


def on_device(vorticity, position, counts, owner_ids, slot_ids, velocity):
    leaving = depart(vorticity, position, counts)
    arrivals = [
        stepped(leaving[0], "gx", 1),
        stepped(leaving[1], "gx", -1),
        stepped(leaving[2], "gz", 1),
        stepped(leaving[3], "gz", -1),
    ]
    places, marks = plan(owner_ids[:, 0], slot_ids)
    marks = exchange(marks.reshape(128, 1, 4)).reshape(512)
    ship = route(places, vorticity, position, counts, arrivals)
    rows = exchange(ship.reshape(128, 24, 128)).reshape(3072, 128)

    vel = jnp.transpose(velocity, (0, 1, 3, 2, 4))
    xb = stepped(vel[3], "gx", 1)
    xa = stepped(vel[0], "gx", -1)
    zb = stepped(vel[:, :, :, 15:], "gz", 1)
    za = stepped(vel[:, :, :, :1], "gz", -1)
    grads = gradient(vel, xb, xa, zb, za)

    mesh, back = owner_work(marks, rows, grads)
    back = exchange(back.reshape(128, 3, 4, 128)).reshape(1536, 128)
    stretching = unpack(places, back)
    mesh = jnp.transpose(mesh.reshape(4, 16, 3, 16, 128), (0, 1, 3, 2, 4))
    return mesh, stretching


def solution(mesh):
    placed = (
        P(None, None, AXES),
        P(None, None, AXES),
        P(None, AXES),
        P(AXES, None),
        P(AXES),
        P("gx", None, "gz", None, None),
    )
    return jax.shard_map(
        on_device,
        mesh=mesh,
        in_specs=placed,
        out_specs=(P("gx", None, "gz", None, None), P(None, None, None, AXES)),
        check_vma=False,
    )
```

```python
import jax
import jax.numpy as jnp
import numpy as np
from jax import lax
from jax.experimental import pallas as pl
from jax.experimental.pallas import tpu as pltpu
from jax.sharding import PartitionSpec as P

AXES = ("gx", "gz")
F32 = jnp.float32
BF16 = jnp.bfloat16
VMEM = pl.BlockSpec(memory_space=pltpu.VMEM)
SMEM = pl.BlockSpec(memory_space=pltpu.SMEM)
ANY = pl.BlockSpec(memory_space=pl.ANY)
PARAMS = pltpu.CompilerParams(vmem_limit_bytes=16 * 1024 * 1024)
GRAD_ROWS = 64 * 9 * 16
GRAD_PAD = 128
GROUP = 8


def sds(shape, dtype=F32):
    return jax.ShapeDtypeStruct(shape, dtype)


def cost(flops, read):
    return pl.CostEstimate(flops=flops, bytes_accessed=read, transcendentals=0)


def depart_kernel(vort, pos, counts, d0, d1, d2, d3, v_here, p_here, c_here, sems):
    copies = [
        pltpu.make_async_copy(source, target, sems.at[n])
        for n, (source, target) in enumerate(((counts, c_here), (vort, v_here), (pos, p_here)))
    ]
    for copy in copies:
        copy.start()
    for copy in copies:
        copy.wait()
    place = lax.broadcasted_iota(jnp.int32, (32, 128), 0)
    for heading, out in enumerate((d0, d1, d2, d3)):
        leaves = place < c_here[heading : heading + 1, :]
        rows = slice(heading * 32, heading * 32 + 32)
        for i in range(3):
            out[i] = jnp.where(leaves, v_here[i, rows, :], 0.0)
            out[3 + i] = jnp.where(leaves, p_here[i, rows, :], 0.0)


def depart(vort, pos, counts):
    return pl.pallas_call(
        depart_kernel,
        out_shape=[sds((6, 32, 128))] * 4,
        in_specs=[ANY] * 3,
        out_specs=[VMEM] * 4,
        scratch_shapes=[
            pltpu.VMEM((3, 128, 128), F32),
            pltpu.VMEM((3, 128, 128), F32),
            pltpu.VMEM((4, 128), jnp.int32),
            pltpu.SemaphoreType.DMA((3,)),
        ],
        compiler_params=PARAMS,
        cost_estimate=cost(400_000, 1_600_000),
        name="depart",
    )(vort, pos, counts)


ORDER = (3, 4, 0, 1, 2, 5)


def send_rows(places, turned, ship, first):
    def move(r, carry):
        place = places[first + r]
        base = (place >> 2) * 28 + (place & 3)
        ship[pl.ds(base, 7, stride=4), :] = turned[pl.ds(r, 7, stride=128), :]
        return carry

    lax.fori_loop(0, 128, move, 0, unroll=8)


def slot_rows(slots, half, turned):
    row = slots[half : half + 1, :].astype(F32)
    turned[768:896, :] = jnp.broadcast_to(row, (128, 128)).T


def keep_kernel(owners, vort, pos, counts, slots, places, turned, tally):
    for i in range(128):
        tally[i] = 0

    def rank_of(r, carry):
        owner = owners[r]
        rank = tally[owner]
        tally[owner] = rank + 1
        places[r] = owner * 4 + rank
        return carry

    lax.fori_loop(0, 256, rank_of, 0, unroll=8)
    place = lax.broadcasted_iota(jnp.int32, (32, 128), 0)
    leaves = [place < counts[heading : heading + 1, :] for heading in range(4)]
    for at, comp in enumerate(ORDER):
        if comp < 3:
            kept = jnp.concatenate(
                [
                    jnp.where(leaves[h], 0.0, vort[comp, 32 * h : 32 * h + 32, :])
                    for h in range(4)
                ],
                axis=0,
            )
        else:
            kept = pos[comp - 3]
        turned[at * 128 : at * 128 + 128, :] = kept.T
    slot_rows(slots, 0, turned)


def keep(owners, vort, pos, counts, slots):
    return pl.pallas_call(
        keep_kernel,
        out_shape=[sds((256,), jnp.int32), sds((896, 128))],
        in_specs=[SMEM] + [VMEM] * 4,
        out_specs=[SMEM, VMEM],
        scratch_shapes=[pltpu.SMEM((128,), jnp.int32)],
        compiler_params=PARAMS,
        cost_estimate=cost(1_000_000, 4_000_000),
        name="keep",
    )(owners, vort, pos, counts, slots)


def route_kernel(places, slots, a0, a1, a2, a3, kept, ship, turned):
    def clear(i, carry):
        ship[pl.ds(pl.multiple_of(i * 64, 64), 64), :] = jnp.zeros((64, 128), F32)
        return carry

    lax.fori_loop(0, 56, clear, 0)
    send_rows(places, kept, ship, 0)
    for at, comp in enumerate(ORDER):
        came = jnp.concatenate([a[comp] for a in (a0, a1, a2, a3)], axis=0)
        turned[at * 128 : at * 128 + 128, :] = came.T
    slot_rows(slots, 1, turned)
    send_rows(places, turned, ship, 128)


def route(places, slots, arrivals, kept):
    return pl.pallas_call(
        route_kernel,
        out_shape=sds((3584, 128)),
        in_specs=[SMEM] + [VMEM] * 6,
        out_specs=VMEM,
        scratch_shapes=[pltpu.VMEM((896, 128), F32)],
        compiler_params=PARAMS,
        cost_estimate=cost(1_000_000, 4_000_000),
        name="route",
    )(places, slots, *arrivals, kept)


def stencil(stride, per):
    here, before, after = (np.zeros((128, 128), np.float32) for _ in range(3))
    factors = {1: 45.0, -1: -45.0, 2: -9.0, -2: 9.0, 3: 1.0, -3: -1.0}
    for lane in range(128):
        digit = lane // stride % per
        for offset, factor in factors.items():
            at = lane + offset * stride
            if digit + offset >= per:
                after[at - per * stride, lane] = factor
            elif digit + offset < 0:
                before[at + per * stride, lane] = factor
            else:
                here[at, lane] = factor
    return here, before, after


def matrices():
    along_x = np.concatenate(stencil(32, 4) * 2)
    along_y = np.concatenate(stencil(8, 4) * 2)
    here, before, after = stencil(1, 8)
    along_z = np.concatenate((here, before + after) * 2)
    return [jnp.asarray(m, BF16) for m in (along_x, along_y, along_z)]


def split(value):
    high = value.astype(BF16)
    return high, (value - high.astype(F32)).astype(BF16)


def gradient_kernel(vel, xb, xa, zb, za, mx, my, mz, out, high, low, z_high, z_low):
    late = lax.broadcasted_iota(jnp.int32, (16, 128), 1) % 8 >= 5

    def put(sx, sy, value):
        at = pl.ds(pl.multiple_of((sx * 18 + sy) * 48, 16), 48)
        high[at, :], low[at, :] = split(value)

    def fill(sy, carry):
        rows = pl.ds(pl.multiple_of(sy * 48, 16), 48)
        put(0, sy + 1, xb[rows, :])
        put(5, sy + 1, xa[rows, :])
        for sx in range(4):
            row = (sx * 16 + sy) * 48
            value = vel[pl.ds(pl.multiple_of(row, 16), 48), :]
            put(sx + 1, sy + 1, value)
            for i in range(3):
                c = value[16 * i : 16 * i + 16]
                edge = pl.ds((sx * 16 + sy) * 3 + i, 1)
                before = jnp.concatenate([zb[edge, :], c[:15]], axis=0)
                after = jnp.concatenate([c[1:], za[edge, :]], axis=0)
                at = pl.ds(pl.multiple_of(row + 16 * i, 16), 16)
                z_high[at, :], z_low[at, :] = split(jnp.where(late, before, after))
        return carry

    lax.fori_loop(0, 16, fill, 0)
    for sx in range(4):
        put(sx + 1, 0, vel[(sx * 16 + 15) * 48 : (sx * 16 + 16) * 48, :])
        put(sx + 1, 17, vel[sx * 16 * 48 : (sx * 16 + 1) * 48, :])

    def per_x(sx, carry):
        def part(ref, dx, dy):
            at = pl.multiple_of(((sx + 1 + dx) * 18 + 1 + dy) * 48, 16)
            return ref[pl.ds(at, 768), :]

        both = (high, low)
        own = pl.ds(pl.multiple_of(sx * 768, 16), 768)
        along_x = [part(ref, dx, 0) for ref in both for dx in (0, -1, 1)]
        along_y = [part(ref, 0, dy) for ref in both for dy in (0, -1, 1)]
        along_z = [part(high, 0, 0), z_high[own, :], part(low, 0, 0), z_low[own, :]]
        for j, (parts, matrix) in enumerate(((along_x, mx), (along_y, my), (along_z, mz))):
            value = jnp.dot(
                jnp.concatenate(parts, axis=1), matrix[...], preferred_element_type=F32
            ) * (1.0 / 60.0)
            for sy in range(16):
                at = pl.multiple_of(((sx * 16 + sy) * 9 + 3 * j) * 16, 16)
                out[pl.ds(at, 48), :] = value[48 * sy : 48 * sy + 48]
        return carry

    lax.fori_loop(0, 4, per_x, 0)
    out[GRAD_ROWS:, :] = jnp.zeros((GRAD_PAD, 128), F32)


def gradient(vel, xb, xa, zb, za):
    return pl.pallas_call(
        gradient_kernel,
        out_shape=sds((GRAD_ROWS + GRAD_PAD, 128)),
        in_specs=[VMEM] * 8,
        out_specs=VMEM,
        scratch_shapes=[pltpu.VMEM((6 * 18 * 48, 128), BF16)] * 2
        + [pltpu.VMEM((3072, 128), BF16)] * 2,
        compiler_params=PARAMS,
        cost_estimate=cost(20_000_000, 8_000_000),
        name="gradient",
    )(vel, xb, xa, zb, za, *matrices())


def owner_kernel(rows, grads, mesh, back):
    def clear(i, carry):
        mesh[pl.ds(pl.multiple_of(i * 64, 64), 64), :] = jnp.zeros((64, 128), F32)
        return carry

    lax.fori_loop(0, 48, clear, 0)
    cell_z = lax.broadcasted_iota(jnp.int32, (8, 128), 0).astype(F32)

    def wide(row):
        return jnp.broadcast_to(row, (8, 128))

    def per_source(s, base):
        f = rows[pl.ds(base, 8), :] - 1.0
        g = 1.0 - f
        weights = (
            -0.5 * f * g * g,
            1.0 + f * f * (1.5 * f - 2.5),
            1.0 + g * g * (1.5 * g - 2.5),
            -0.5 * g * f * f,
        )
        slots = rows[pl.ds(base + 24, 4), :].astype(jnp.int32)
        for k in range(4):
            slot = slots[k, 0]
            column = slot >> 4
            level = slot & 15
            z = wide(rows[pl.ds(base + 20 + k, 1), :])
            radius = jnp.abs(cell_z - z)
            rest = jnp.maximum(2.0 - radius, 0.0)
            along_z = jnp.where(
                radius < 1.0,
                1.0 + radius * radius * (1.5 * radius - 2.5),
                0.5 * rest * rest * (1.0 - radius),
            )
            yz = [wide(weights[b][4 + k : 5 + k]) * along_z for b in range(4)]
            xs = [wide(weights[a][k : k + 1]) for a in range(4)]
            table = jnp.concatenate([xs[a] * yz[b] for a in range(4) for b in range(4)], axis=0)
            high, low = split(table)

            vortex = [rows[pl.ds(base + 8 + 4 * j + k, 1), :] for j in range(3)]
            grad = jnp.concatenate(
                [
                    grads[pl.ds(column * 144 + j * 48 + level, 8, stride=16), :]
                    for j in range(3)
                ],
                axis=0,
            )
            left = jnp.concatenate(split(grad), axis=0)
            left = jnp.concatenate([left, left], axis=1)
            sampled = jnp.dot(
                left, jnp.concatenate([high, low], axis=0), preferred_element_type=F32
            )
            sampled = sampled[:24] + sampled[24:]
            stretch = (
                sampled[0:8] * wide(vortex[0])
                + sampled[8:16] * wide(vortex[1])
                + sampled[16:24] * wide(vortex[2])
            )
            back[pl.ds(s * 12 + k, 3, stride=4), :] = stretch[:3]

            v = jnp.concatenate(vortex + [jnp.zeros((5, 128), F32)], axis=0)
            left = jnp.concatenate(split(v), axis=0)
            left = jnp.concatenate([left, left], axis=1)
            patch = lax.dot_general(
                left,
                jnp.concatenate([high, low], axis=1),
                (((1,), (1,)), ((), ())),
                preferred_element_type=F32,
            )
            patch = patch[:3] + patch[8:11]
            at = pl.ds(column * 48 + level, 3, stride=16)
            mesh[at, :] = mesh[at, :] + patch

    def per_group(q, carry):
        base = pl.multiple_of(q * (28 * GROUP), 8)
        for u in range(GROUP):
            per_source(q * GROUP + u, base + 28 * u)
        return carry

    lax.fori_loop(0, 128 // GROUP, per_group, 0)


def owner_work(rows, grads):
    return pl.pallas_call(
        owner_kernel,
        out_shape=[sds((3072, 128)), sds((1536, 128))],
        in_specs=[VMEM, VMEM],
        out_specs=[VMEM] * 2,
        compiler_params=PARAMS,
        cost_estimate=cost(300_000_000, 9_000_000),
        name="owner",
    )(rows, grads)


def unpack_kernel(places, back, out, turned):
    def move(r, carry):
        place = places[r]
        base = (place >> 2) * 12 + (place & 3)
        turned[pl.ds(r, 3, stride=256), :] = back[pl.ds(base, 3, stride=4), :]
        return carry

    lax.fori_loop(0, 256, move, 0, unroll=8)
    for h in range(2):
        for i in range(3):
            at = i * 256 + h * 128
            out[h, i] = turned[at : at + 128, :].T


def unpack(places, back):
    return pl.pallas_call(
        unpack_kernel,
        out_shape=sds((2, 3, 128, 128)),
        in_specs=[SMEM, VMEM],
        out_specs=VMEM,
        scratch_shapes=[pltpu.VMEM((768, 128), F32)],
        compiler_params=PARAMS,
        cost_estimate=cost(1_000_000, 2_000_000),
        name="unpack",
    )(places, back)


def stepped(value, axis, step):
    count = lax.axis_size(axis)
    first, last = (max(0, -step), min(count, count - step))
    return lax.ppermute(value, axis, [(source, source + step) for source in range(first, last)])


def exchange(value):
    return lax.all_to_all(value, AXES, split_axis=0, concat_axis=0, tiled=True)


def on_device(vorticity, position, counts, owner_ids, slot_ids, velocity):
    slots = slot_ids.reshape(2, 128)
    leaving = depart(vorticity, position, counts)
    arrivals = [
        stepped(leaving[0], "gx", 1),
        stepped(leaving[1], "gx", -1),
        stepped(leaving[2], "gz", 1),
        stepped(leaving[3], "gz", -1),
    ]
    places, kept = keep(owner_ids[:, 0], vorticity, position, counts, slots)
    ship = route(places, slots, arrivals, kept)
    rows = exchange(ship.reshape(128, 7, 4, 128)).reshape(3584, 128)

    vel = jnp.transpose(velocity, (0, 1, 3, 2, 4))
    xb = stepped(vel[3].reshape(768, 128), "gx", 1)
    xa = stepped(vel[0].reshape(768, 128), "gx", -1)
    zb = stepped(vel[:, :, :, 15].reshape(192, 128), "gz", 1)
    za = stepped(vel[:, :, :, 0].reshape(192, 128), "gz", -1)
    grads = gradient(vel.reshape(3072, 128), xb, xa, zb, za)

    mesh, back = owner_work(rows, grads)
    back = exchange(back.reshape(128, 3, 4, 128)).reshape(1536, 128)
    stretching = unpack(places, back)
    mesh = jnp.transpose(mesh.reshape(4, 16, 3, 16, 128), (0, 1, 3, 2, 4))
    return mesh, stretching


def solution(mesh):
    placed = (
        P(None, None, AXES),
        P(None, None, AXES),
        P(None, AXES),
        P(AXES, None),
        P(AXES),
        P("gx", None, "gz", None, None),
    )
    return jax.shard_map(
        on_device,
        mesh=mesh,
        in_specs=placed,
        out_specs=(P("gx", None, "gz", None, None), P(None, None, None, AXES)),
        check_vma=False,
    )
```

```python
import jax
import jax.numpy as jnp
import numpy as np
from jax import lax
from jax.experimental import pallas as pl
from jax.experimental.pallas import tpu as pltpu
from jax.sharding import PartitionSpec as P

AXES = ("gx", "gz")
F32 = jnp.float32
BF16 = jnp.bfloat16
VMEM = pl.BlockSpec(memory_space=pltpu.VMEM)
SMEM = pl.BlockSpec(memory_space=pltpu.SMEM)
ANY = pl.BlockSpec(memory_space=pl.ANY)
PARAMS = pltpu.CompilerParams(vmem_limit_bytes=16 * 1024 * 1024)
LARGE = pltpu.CompilerParams(vmem_limit_bytes=60 * 1024 * 1024)
GRAD_ROWS = 64 * 9 * 16
GRAD_PAD = 128
GROUP = 8


def sds(shape, dtype=F32):
    return jax.ShapeDtypeStruct(shape, dtype)


def cost(flops, read):
    return pl.CostEstimate(flops=flops, bytes_accessed=read, transcendentals=0)


def depart_kernel(vort, pos, counts, vel, d0, d1, d2, d3, v_here, p_here, c_here, u_here, out, sems):
    layer = pl.ds(192, 768)
    fetches = [
        pltpu.make_async_copy(source, target, sems.at[n])
        for n, (source, target) in enumerate(
            ((counts, c_here), (vort, v_here), (pos, p_here), (vel, u_here))
        )
    ]
    sides = [
        pltpu.make_async_copy(u_here.at[pl.ds(3 * 768, 768), :], d0.at[layer, :], sems.at[4]),
        pltpu.make_async_copy(u_here.at[pl.ds(0, 768), :], d1.at[layer, :], sems.at[5]),
    ]
    for copy in fetches:
        copy.start()
    for copy in fetches[:3]:
        copy.wait()
    place = lax.broadcasted_iota(jnp.int32, (32, 128), 0)
    sends = []
    for heading in range(4):
        leaves = place < c_here[heading : heading + 1, :]
        rows = slice(heading * 32, heading * 32 + 32)
        for i in range(3):
            out[heading, 32 * i : 32 * i + 32, :] = jnp.where(leaves, v_here[i, rows, :], 0.0)
            out[heading, 96 + 32 * i : 128 + 32 * i, :] = jnp.where(leaves, p_here[i, rows, :], 0.0)
        if heading < 2:
            target = (d0, d1)[heading].at[pl.ds(0, 192), :]
            sends.append(
                pltpu.make_async_copy(
                    out.at[heading, pl.ds(0, 192), :], target, sems.at[6 + heading]
                )
            )
            sends[-1].start()
    fetches[3].wait()
    for copy in sides:
        copy.start()
    for heading, level in ((2, 15), (3, 0)):
        out[heading, 192:384, :] = u_here[pl.ds(level, 192, stride=16), :]
        target = (d2, d3)[heading - 2]
        sends.append(pltpu.make_async_copy(out.at[heading], target, sems.at[6 + heading]))
        sends[-1].start()
    for copy in sides + sends:
        copy.wait()


def depart(vort, pos, counts, vel):
    return pl.pallas_call(
        depart_kernel,
        out_shape=[sds((960, 128))] * 2 + [sds((384, 128))] * 2,
        in_specs=[ANY] * 4,
        out_specs=[ANY] * 4,
        scratch_shapes=[
            pltpu.VMEM((3, 128, 128), F32),
            pltpu.VMEM((3, 128, 128), F32),
            pltpu.VMEM((4, 128), jnp.int32),
            pltpu.VMEM((3072, 128), F32),
            pltpu.VMEM((4, 384, 128), F32),
            pltpu.SemaphoreType.DMA((10,)),
        ],
        compiler_params=LARGE,
        cost_estimate=cost(400_000, 3_000_000),
        name="depart",
    )(vort, pos, counts, vel)


ORDER = (3, 4, 0, 1, 2, 5)


def send_rows(places, turned, ship, first):
    def move(r, carry):
        place = places[first + r]
        base = (place >> 2) * 28 + (place & 3)
        ship[pl.ds(base, 7, stride=4), :] = turned[pl.ds(r, 7, stride=128), :]
        return carry

    lax.fori_loop(0, 128, move, 0, unroll=8)


def slot_rows(slots, half, turned):
    row = slots[half : half + 1, :].astype(F32)
    turned[768:896, :] = jnp.broadcast_to(row, (128, 128)).T


def keep_kernel(
    owners, vort, pos, counts, slots, places, turned, tally, v_here, p_here, c_here, s_here, sems
):
    fetches = [
        pltpu.make_async_copy(source, target, sems.at[n])
        for n, (source, target) in enumerate(
            ((counts, c_here), (vort, v_here), (pos, p_here), (slots, s_here))
        )
    ]
    for copy in fetches:
        copy.start()
    for i in range(128):
        tally[i] = 0

    def rank_of(r, carry):
        owner = owners[r]
        rank = tally[owner]
        tally[owner] = rank + 1
        places[r] = owner * 4 + rank
        return carry

    lax.fori_loop(0, 256, rank_of, 0, unroll=8)
    for copy in fetches:
        copy.wait()
    place = lax.broadcasted_iota(jnp.int32, (32, 128), 0)
    leaves = [place < c_here[heading : heading + 1, :] for heading in range(4)]
    for at, comp in enumerate(ORDER):
        if comp < 3:
            kept = jnp.concatenate(
                [
                    jnp.where(leaves[h], 0.0, v_here[comp, 32 * h : 32 * h + 32, :])
                    for h in range(4)
                ],
                axis=0,
            )
        else:
            kept = p_here[comp - 3]
        turned[at * 128 : at * 128 + 128, :] = kept.T
    slot_rows(s_here, 0, turned)


def keep(owners, vort, pos, counts, slots):
    return pl.pallas_call(
        keep_kernel,
        out_shape=[sds((256,), jnp.int32), sds((896, 128))],
        in_specs=[SMEM] + [ANY] * 4,
        out_specs=[SMEM, VMEM],
        scratch_shapes=[
            pltpu.SMEM((128,), jnp.int32),
            pltpu.VMEM((3, 128, 128), F32),
            pltpu.VMEM((3, 128, 128), F32),
            pltpu.VMEM((4, 128), jnp.int32),
            pltpu.VMEM((2, 128), jnp.int32),
            pltpu.SemaphoreType.DMA((4,)),
        ],
        compiler_params=LARGE,
        cost_estimate=cost(1_000_000, 4_000_000),
        name="keep",
    )(owners, vort, pos, counts, slots)


def route_kernel(places, slots, a0, a1, a2, a3, kept, ship, turned):
    def clear(i, carry):
        ship[pl.ds(pl.multiple_of(i * 64, 64), 64), :] = jnp.zeros((64, 128), F32)
        return carry

    lax.fori_loop(0, 56, clear, 0)
    send_rows(places, kept, ship, 0)
    for at, comp in enumerate(ORDER):
        came = jnp.concatenate(
            [a[32 * comp : 32 * comp + 32, :] for a in (a0, a1, a2, a3)], axis=0
        )
        turned[at * 128 : at * 128 + 128, :] = came.T
    slot_rows(slots, 1, turned)
    send_rows(places, turned, ship, 128)


def route(places, slots, arrivals, kept):
    return pl.pallas_call(
        route_kernel,
        out_shape=sds((3584, 128)),
        in_specs=[SMEM] + [VMEM] * 6,
        out_specs=VMEM,
        scratch_shapes=[pltpu.VMEM((896, 128), F32)],
        compiler_params=PARAMS,
        cost_estimate=cost(1_000_000, 4_000_000),
        name="route",
    )(places, slots, *arrivals, kept)


def stencil(stride, per):
    here, before, after = (np.zeros((128, 128), np.float32) for _ in range(3))
    factors = {1: 45.0, -1: -45.0, 2: -9.0, -2: 9.0, 3: 1.0, -3: -1.0}
    for lane in range(128):
        digit = lane // stride % per
        for offset, factor in factors.items():
            at = lane + offset * stride
            if digit + offset >= per:
                after[at - per * stride, lane] = factor
            elif digit + offset < 0:
                before[at + per * stride, lane] = factor
            else:
                here[at, lane] = factor
    return here, before, after


def matrices():
    along_x = np.concatenate(stencil(32, 4) * 2)
    along_y = np.concatenate(stencil(8, 4) * 2)
    here, before, after = stencil(1, 8)
    along_z = np.concatenate((here, before + after) * 2)
    return [jnp.asarray(m, BF16) for m in (along_x, along_y, along_z)]


def split(value):
    high = value.astype(BF16)
    return high, (value - high.astype(F32)).astype(BF16)


def gradient_kernel(vel, xb, xa, zb, za, mx, my, mz, out, high, low, z_high, z_low):
    late = lax.broadcasted_iota(jnp.int32, (16, 128), 1) % 8 >= 5

    def put(sx, sy, value):
        at = pl.ds(pl.multiple_of((sx * 18 + sy) * 48, 16), 48)
        high[at, :], low[at, :] = split(value)

    def fill(sy, carry):
        rows = pl.ds(pl.multiple_of(192 + sy * 48, 16), 48)
        put(0, sy + 1, xb[rows, :])
        put(5, sy + 1, xa[rows, :])
        for sx in range(4):
            row = (sx * 16 + sy) * 48
            value = vel[pl.ds(pl.multiple_of(row, 16), 48), :]
            put(sx + 1, sy + 1, value)
            for i in range(3):
                c = value[16 * i : 16 * i + 16]
                edge = pl.ds(192 + (sx * 16 + sy) * 3 + i, 1)
                before = jnp.concatenate([zb[edge, :], c[:15]], axis=0)
                after = jnp.concatenate([c[1:], za[edge, :]], axis=0)
                at = pl.ds(pl.multiple_of(row + 16 * i, 16), 16)
                z_high[at, :], z_low[at, :] = split(jnp.where(late, before, after))
        return carry

    lax.fori_loop(0, 16, fill, 0)
    for sx in range(4):
        put(sx + 1, 0, vel[(sx * 16 + 15) * 48 : (sx * 16 + 16) * 48, :])
        put(sx + 1, 17, vel[sx * 16 * 48 : (sx * 16 + 1) * 48, :])

    def per_x(sx, carry):
        def part(ref, dx, dy):
            at = pl.multiple_of(((sx + 1 + dx) * 18 + 1 + dy) * 48, 16)
            return ref[pl.ds(at, 768), :]

        both = (high, low)
        own = pl.ds(pl.multiple_of(sx * 768, 16), 768)
        along_x = [part(ref, dx, 0) for ref in both for dx in (0, -1, 1)]
        along_y = [part(ref, 0, dy) for ref in both for dy in (0, -1, 1)]
        along_z = [part(high, 0, 0), z_high[own, :], part(low, 0, 0), z_low[own, :]]
        for j, (parts, matrix) in enumerate(((along_x, mx), (along_y, my), (along_z, mz))):
            value = jnp.dot(
                jnp.concatenate(parts, axis=1), matrix[...], preferred_element_type=F32
            ) * (1.0 / 60.0)
            for sy in range(16):
                at = pl.multiple_of(((sx * 16 + sy) * 9 + 3 * j) * 16, 16)
                out[pl.ds(at, 48), :] = value[48 * sy : 48 * sy + 48]
        return carry

    lax.fori_loop(0, 4, per_x, 0)
    out[GRAD_ROWS:, :] = jnp.zeros((GRAD_PAD, 128), F32)


def gradient(vel, xb, xa, zb, za):
    return pl.pallas_call(
        gradient_kernel,
        out_shape=sds((GRAD_ROWS + GRAD_PAD, 128)),
        in_specs=[VMEM] * 8,
        out_specs=VMEM,
        scratch_shapes=[pltpu.VMEM((6 * 18 * 48, 128), BF16)] * 2
        + [pltpu.VMEM((3072, 128), BF16)] * 2,
        compiler_params=PARAMS,
        cost_estimate=cost(20_000_000, 8_000_000),
        name="gradient",
    )(vel, xb, xa, zb, za, *matrices())


def owner_kernel(rows, grads, mesh, back):
    def clear(i, carry):
        mesh[pl.ds(pl.multiple_of(i * 64, 64), 64), :] = jnp.zeros((64, 128), F32)
        return carry

    lax.fori_loop(0, 48, clear, 0)
    cell_z = lax.broadcasted_iota(jnp.int32, (8, 128), 0).astype(F32)

    def wide(row):
        return jnp.broadcast_to(row, (8, 128))

    def per_source(s, base):
        f = rows[pl.ds(base, 8), :] - 1.0
        g = 1.0 - f
        weights = (
            -0.5 * f * g * g,
            1.0 + f * f * (1.5 * f - 2.5),
            1.0 + g * g * (1.5 * g - 2.5),
            -0.5 * g * f * f,
        )
        slots = rows[pl.ds(base + 24, 4), :].astype(jnp.int32)
        for k in range(4):
            slot = slots[k, 0]
            column = slot >> 4
            level = slot & 15
            z = wide(rows[pl.ds(base + 20 + k, 1), :])
            radius = jnp.abs(cell_z - z)
            rest = jnp.maximum(2.0 - radius, 0.0)
            along_z = jnp.where(
                radius < 1.0,
                1.0 + radius * radius * (1.5 * radius - 2.5),
                0.5 * rest * rest * (1.0 - radius),
            )
            yz = [wide(weights[b][4 + k : 5 + k]) * along_z for b in range(4)]
            xs = [wide(weights[a][k : k + 1]) for a in range(4)]
            table = jnp.concatenate([xs[a] * yz[b] for a in range(4) for b in range(4)], axis=0)
            high, low = split(table)

            vortex = [rows[pl.ds(base + 8 + 4 * j + k, 1), :] for j in range(3)]
            grad = jnp.concatenate(
                [
                    grads[pl.ds(column * 144 + j * 48 + level, 8, stride=16), :]
                    for j in range(3)
                ],
                axis=0,
            )
            left = jnp.concatenate(split(grad), axis=0)
            left = jnp.concatenate([left, left], axis=1)
            sampled = jnp.dot(
                left, jnp.concatenate([high, low], axis=0), preferred_element_type=F32
            )
            sampled = sampled[:24] + sampled[24:]
            stretch = (
                sampled[0:8] * wide(vortex[0])
                + sampled[8:16] * wide(vortex[1])
                + sampled[16:24] * wide(vortex[2])
            )
            back[pl.ds(s * 12 + k, 3, stride=4), :] = stretch[:3]

            v = jnp.concatenate(vortex + [jnp.zeros((5, 128), F32)], axis=0)
            left = jnp.concatenate(split(v), axis=0)
            left = jnp.concatenate([left, left], axis=1)
            patch = lax.dot_general(
                left,
                jnp.concatenate([high, low], axis=1),
                (((1,), (1,)), ((), ())),
                preferred_element_type=F32,
            )
            patch = patch[:3] + patch[8:11]
            at = pl.ds(column * 48 + level, 3, stride=16)
            mesh[at, :] = mesh[at, :] + patch

    def per_group(q, carry):
        base = pl.multiple_of(q * (28 * GROUP), 8)
        for u in range(GROUP):
            per_source(q * GROUP + u, base + 28 * u)
        return carry

    lax.fori_loop(0, 128 // GROUP, per_group, 0)


def owner_work(rows, grads):
    return pl.pallas_call(
        owner_kernel,
        out_shape=[sds((3072, 128)), sds((1536, 128))],
        in_specs=[VMEM, VMEM],
        out_specs=[VMEM] * 2,
        compiler_params=PARAMS,
        cost_estimate=cost(300_000_000, 9_000_000),
        name="owner",
    )(rows, grads)


def unpack_kernel(places, back, out, turned):
    def move(r, carry):
        place = places[r]
        base = (place >> 2) * 12 + (place & 3)
        turned[pl.ds(r, 3, stride=256), :] = back[pl.ds(base, 3, stride=4), :]
        return carry

    lax.fori_loop(0, 256, move, 0, unroll=8)
    for h in range(2):
        for i in range(3):
            at = i * 256 + h * 128
            out[h, i] = turned[at : at + 128, :].T


def unpack(places, back):
    return pl.pallas_call(
        unpack_kernel,
        out_shape=sds((2, 3, 128, 128)),
        in_specs=[SMEM, VMEM],
        out_specs=VMEM,
        scratch_shapes=[pltpu.VMEM((768, 128), F32)],
        compiler_params=PARAMS,
        cost_estimate=cost(1_000_000, 2_000_000),
        name="unpack",
    )(places, back)


def stepped(value, axis, step):
    count = lax.axis_size(axis)
    first, last = (max(0, -step), min(count, count - step))
    return lax.ppermute(value, axis, [(source, source + step) for source in range(first, last)])


def exchange(value):
    return lax.all_to_all(value, AXES, split_axis=0, concat_axis=0, tiled=True)


def on_device(vorticity, position, counts, owner_ids, slot_ids, velocity):
    slots = slot_ids.reshape(2, 128)
    vel = jnp.transpose(velocity, (0, 1, 3, 2, 4)).reshape(3072, 128)
    leaving = depart(vorticity, position, counts, vel)
    arrivals = [
        stepped(leaving[0], "gx", 1),
        stepped(leaving[1], "gx", -1),
        stepped(leaving[2], "gz", 1),
        stepped(leaving[3], "gz", -1),
    ]
    places, kept = keep(owner_ids[:, 0], vorticity, position, counts, slots)
    ship = route(places, slots, arrivals, kept)
    rows = exchange(ship.reshape(128, 7, 4, 128)).reshape(3584, 128)

    grads = gradient(vel, *arrivals)

    mesh, back = owner_work(rows, grads)
    back = exchange(back.reshape(128, 3, 4, 128)).reshape(1536, 128)
    stretching = unpack(places, back)
    mesh = jnp.transpose(mesh.reshape(4, 16, 3, 16, 128), (0, 1, 3, 2, 4))
    return mesh, stretching


def solution(mesh):
    placed = (
        P(None, None, AXES),
        P(None, None, AXES),
        P(None, AXES),
        P(AXES, None),
        P(AXES),
        P("gx", None, "gz", None, None),
    )
    return jax.shard_map(
        on_device,
        mesh=mesh,
        in_specs=placed,
        out_specs=(P("gx", None, "gz", None, None), P(None, None, None, AXES)),
        check_vma=False,
    )
```

```python
import jax
import jax.numpy as jnp
import numpy as np
from jax import lax
from jax.experimental import pallas as pl
from jax.experimental.pallas import tpu as pltpu
from jax.sharding import PartitionSpec as P

AXES = ("gx", "gz")
F32 = jnp.float32
BF16 = jnp.bfloat16
VMEM = pl.BlockSpec(memory_space=pltpu.VMEM)
SMEM = pl.BlockSpec(memory_space=pltpu.SMEM)
ANY = pl.BlockSpec(memory_space=pl.ANY)
PARAMS = pltpu.CompilerParams(vmem_limit_bytes=16 * 1024 * 1024)
LARGE = pltpu.CompilerParams(vmem_limit_bytes=60 * 1024 * 1024)
GRAD_ROWS = 64 * 9 * 16
GRAD_PAD = 128
GROUP = 8
EARLY = 2


def sds(shape, dtype=F32):
    return jax.ShapeDtypeStruct(shape, dtype)


def cost(flops, read):
    return pl.CostEstimate(flops=flops, bytes_accessed=read, transcendentals=0)


def depart_kernel(vort, pos, counts, vel, d0, d1, d2, d3, v_here, p_here, c_here, u_here, out, sems):
    layer = pl.ds(192, 768)
    fetches = [
        pltpu.make_async_copy(source, target, sems.at[n])
        for n, (source, target) in enumerate(
            ((counts, c_here), (vort, v_here), (pos, p_here), (vel, u_here))
        )
    ]
    sides = [
        pltpu.make_async_copy(u_here.at[pl.ds(3 * 768, 768), :], d0.at[layer, :], sems.at[4]),
        pltpu.make_async_copy(u_here.at[pl.ds(0, 768), :], d1.at[layer, :], sems.at[5]),
    ]
    for copy in fetches:
        copy.start()
    for copy in fetches[:3]:
        copy.wait()
    place = lax.broadcasted_iota(jnp.int32, (32, 128), 0)
    sends = []
    for heading in range(4):
        leaves = place < c_here[heading : heading + 1, :]
        rows = slice(heading * 32, heading * 32 + 32)
        for i in range(3):
            out[heading, 32 * i : 32 * i + 32, :] = jnp.where(leaves, v_here[i, rows, :], 0.0)
            out[heading, 96 + 32 * i : 128 + 32 * i, :] = jnp.where(leaves, p_here[i, rows, :], 0.0)
        if heading < 2:
            target = (d0, d1)[heading].at[pl.ds(0, 192), :]
            sends.append(
                pltpu.make_async_copy(
                    out.at[heading, pl.ds(0, 192), :], target, sems.at[6 + heading]
                )
            )
            sends[-1].start()
    fetches[3].wait()
    for copy in sides:
        copy.start()
    for heading, level in ((2, 15), (3, 0)):
        out[heading, 192:384, :] = u_here[pl.ds(level, 192, stride=16), :]
        target = (d2, d3)[heading - 2]
        sends.append(pltpu.make_async_copy(out.at[heading], target, sems.at[6 + heading]))
        sends[-1].start()
    for copy in sides + sends:
        copy.wait()


def depart(vort, pos, counts, vel):
    return pl.pallas_call(
        depart_kernel,
        out_shape=[sds((960, 128))] * 2 + [sds((384, 128))] * 2,
        in_specs=[ANY] * 4,
        out_specs=[ANY] * 4,
        scratch_shapes=[
            pltpu.VMEM((3, 128, 128), F32),
            pltpu.VMEM((3, 128, 128), F32),
            pltpu.VMEM((4, 128), jnp.int32),
            pltpu.VMEM((3072, 128), F32),
            pltpu.VMEM((4, 384, 128), F32),
            pltpu.SemaphoreType.DMA((10,)),
        ],
        compiler_params=LARGE,
        cost_estimate=cost(400_000, 3_000_000),
        name="depart",
    )(vort, pos, counts, vel)


ORDER = (3, 4, 0, 1, 2, 5)


def send_rows(places, turned, ship, first):
    lane = lax.broadcasted_iota(jnp.int32, (1, 128), 1)

    def move(r, carry):
        place = places[first + r]
        base = (place >> 2) * 25
        rank = place & 3
        ship[pl.ds(base + rank, 6, stride=4), :] = turned[pl.ds(r, 6, stride=128), :]
        marks = pl.ds(base + 24, 1)
        slot = turned[pl.ds(768 + r, 1), :]
        ship[marks, :] = jnp.where(lane == rank, slot, ship[marks, :])
        return carry

    lax.fori_loop(0, 128, move, 0, unroll=8)


def slot_rows(slots, half, turned):
    row = slots[half : half + 1, :].astype(F32)
    turned[768:896, :] = jnp.broadcast_to(row, (128, 128)).T


def keep_kernel(
    owners, vort, pos, counts, slots, places, turned, tally, v_here, p_here, c_here, s_here, sems
):
    fetches = [
        pltpu.make_async_copy(source, target, sems.at[n])
        for n, (source, target) in enumerate(
            ((counts, c_here), (vort, v_here), (pos, p_here), (slots, s_here))
        )
    ]
    for copy in fetches:
        copy.start()
    for i in range(128):
        tally[i] = 0

    def rank_of(r, carry):
        owner = owners[r]
        rank = tally[owner]
        tally[owner] = rank + 1
        places[r] = owner * 4 + rank
        return carry

    lax.fori_loop(0, 256, rank_of, 0, unroll=8)
    for copy in fetches:
        copy.wait()
    place = lax.broadcasted_iota(jnp.int32, (32, 128), 0)
    leaves = [place < c_here[heading : heading + 1, :] for heading in range(4)]
    for at, comp in enumerate(ORDER):
        if comp < 3:
            kept = jnp.concatenate(
                [
                    jnp.where(leaves[h], 0.0, v_here[comp, 32 * h : 32 * h + 32, :])
                    for h in range(4)
                ],
                axis=0,
            )
        else:
            kept = p_here[comp - 3]
        turned[at * 128 : at * 128 + 128, :] = kept.T
    slot_rows(s_here, 0, turned)


def keep(owners, vort, pos, counts, slots):
    return pl.pallas_call(
        keep_kernel,
        out_shape=[sds((256,), jnp.int32), sds((896, 128))],
        in_specs=[SMEM] + [ANY] * 4,
        out_specs=[SMEM, VMEM],
        scratch_shapes=[
            pltpu.SMEM((128,), jnp.int32),
            pltpu.VMEM((3, 128, 128), F32),
            pltpu.VMEM((3, 128, 128), F32),
            pltpu.VMEM((4, 128), jnp.int32),
            pltpu.VMEM((2, 128), jnp.int32),
            pltpu.SemaphoreType.DMA((4,)),
        ],
        compiler_params=LARGE,
        cost_estimate=cost(1_000_000, 4_000_000),
        name="keep",
    )(owners, vort, pos, counts, slots)


def route_kernel(
    places, slots, a0, a1, a2, a3, kept, ship, turned, kept_here, came_here, s_here, sems
):
    fetches = [
        pltpu.make_async_copy(source.at[pl.ds(0, 192), :], came_here.at[n], sems.at[n])
        for n, source in enumerate((a0, a1, a2, a3))
    ]
    fetches.append(pltpu.make_async_copy(slots, s_here, sems.at[4]))
    fetches.append(pltpu.make_async_copy(kept, kept_here, sems.at[5]))
    for copy in fetches:
        copy.start()

    def clear(i, carry):
        ship[pl.ds(pl.multiple_of(i * 64, 64), 64), :] = jnp.zeros((64, 128), F32)
        return carry

    lax.fori_loop(0, 50, clear, 0)
    fetches[5].wait()
    send_rows(places, kept_here, ship, 0)
    for copy in fetches[:5]:
        copy.wait()
    for at, comp in enumerate(ORDER):
        came = jnp.concatenate(
            [came_here[n, 32 * comp : 32 * comp + 32, :] for n in range(4)], axis=0
        )
        turned[at * 128 : at * 128 + 128, :] = came.T
    slot_rows(s_here, 1, turned)
    send_rows(places, turned, ship, 128)


def route(places, slots, arrivals, kept):
    return pl.pallas_call(
        route_kernel,
        out_shape=sds((3200, 128)),
        in_specs=[SMEM] + [ANY] * 6,
        out_specs=VMEM,
        scratch_shapes=[
            pltpu.VMEM((896, 128), F32),
            pltpu.VMEM((896, 128), F32),
            pltpu.VMEM((4, 192, 128), F32),
            pltpu.VMEM((2, 128), jnp.int32),
            pltpu.SemaphoreType.DMA((6,)),
        ],
        compiler_params=LARGE,
        cost_estimate=cost(1_000_000, 4_000_000),
        name="route",
    )(places, slots, *arrivals, kept)


def stencil(stride, per):
    here, before, after = (np.zeros((128, 128), np.float32) for _ in range(3))
    factors = {1: 45.0, -1: -45.0, 2: -9.0, -2: 9.0, 3: 1.0, -3: -1.0}
    for lane in range(128):
        digit = lane // stride % per
        for offset, factor in factors.items():
            at = lane + offset * stride
            if digit + offset >= per:
                after[at - per * stride, lane] = factor
            elif digit + offset < 0:
                before[at + per * stride, lane] = factor
            else:
                here[at, lane] = factor
    return here, before, after


def matrices():
    along_x = np.concatenate(stencil(32, 4) * 2)
    along_y = np.concatenate(stencil(8, 4) * 2)
    here, before, after = stencil(1, 8)
    along_z = np.concatenate((here, before + after) * 2)
    return [jnp.asarray(m, BF16) for m in (along_x, along_y, along_z)]


def split(value):
    high = value.astype(BF16)
    return high, (value - high.astype(F32)).astype(BF16)


def gradient_kernel(vel, xb, xa, zb, za, mx, my, mz, out, high, low, z_high, z_low):
    late = lax.broadcasted_iota(jnp.int32, (16, 128), 1) % 8 >= 5

    def put(sx, sy, value):
        at = pl.ds(pl.multiple_of((sx * 18 + sy) * 48, 16), 48)
        high[at, :], low[at, :] = split(value)

    def fill(sy, carry):
        rows = pl.ds(pl.multiple_of(192 + sy * 48, 16), 48)
        put(0, sy + 1, xb[rows, :])
        put(5, sy + 1, xa[rows, :])
        for sx in range(4):
            row = (sx * 16 + sy) * 48
            value = vel[pl.ds(pl.multiple_of(row, 16), 48), :]
            put(sx + 1, sy + 1, value)
            for i in range(3):
                c = value[16 * i : 16 * i + 16]
                edge = pl.ds(192 + (sx * 16 + sy) * 3 + i, 1)
                before = jnp.concatenate([zb[edge, :], c[:15]], axis=0)
                after = jnp.concatenate([c[1:], za[edge, :]], axis=0)
                at = pl.ds(pl.multiple_of(row + 16 * i, 16), 16)
                z_high[at, :], z_low[at, :] = split(jnp.where(late, before, after))
        return carry

    lax.fori_loop(0, 16, fill, 0)
    for sx in range(4):
        put(sx + 1, 0, vel[(sx * 16 + 15) * 48 : (sx * 16 + 16) * 48, :])
        put(sx + 1, 17, vel[sx * 16 * 48 : (sx * 16 + 1) * 48, :])

    def per_x(sx, carry):
        def part(ref, dx, dy):
            at = pl.multiple_of(((sx + 1 + dx) * 18 + 1 + dy) * 48, 16)
            return ref[pl.ds(at, 768), :]

        both = (high, low)
        own = pl.ds(pl.multiple_of(sx * 768, 16), 768)
        along_x = [part(ref, dx, 0) for ref in both for dx in (0, -1, 1)]
        along_y = [part(ref, 0, dy) for ref in both for dy in (0, -1, 1)]
        along_z = [part(high, 0, 0), z_high[own, :], part(low, 0, 0), z_low[own, :]]
        for j, (parts, matrix) in enumerate(((along_x, mx), (along_y, my), (along_z, mz))):
            value = jnp.dot(
                jnp.concatenate(parts, axis=1), matrix[...], preferred_element_type=F32
            ) * (1.0 / 60.0)
            for sy in range(16):
                at = pl.multiple_of(((sx * 16 + sy) * 9 + 3 * j) * 16, 16)
                out[pl.ds(at, 48), :] = value[48 * sy : 48 * sy + 48]
        return carry

    lax.fori_loop(0, 4, per_x, 0)
    out[GRAD_ROWS:, :] = jnp.zeros((GRAD_PAD, 128), F32)


def gradient(vel, xb, xa, zb, za):
    return pl.pallas_call(
        gradient_kernel,
        out_shape=sds((GRAD_ROWS + GRAD_PAD, 128)),
        in_specs=[VMEM] * 8,
        out_specs=VMEM,
        scratch_shapes=[pltpu.VMEM((6 * 18 * 48, 128), BF16)] * 2
        + [pltpu.VMEM((3072, 128), BF16)] * 2,
        compiler_params=PARAMS,
        cost_estimate=cost(20_000_000, 8_000_000),
        name="gradient",
    )(vel, xb, xa, zb, za, *matrices())


def wide(row):
    return jnp.broadcast_to(row, (8, 128))


def each_row(rows, work, first, last):
    cell_z = lax.broadcasted_iota(jnp.int32, (8, 128), 0).astype(F32)

    def per_source(s, base):
        f = rows[pl.ds(base, 8), :] - 1.0
        g = 1.0 - f
        weights = (
            -0.5 * f * g * g,
            1.0 + f * f * (1.5 * f - 2.5),
            1.0 + g * g * (1.5 * g - 2.5),
            -0.5 * g * f * f,
        )
        slots = rows[pl.ds(base + 24, 1), :].astype(jnp.int32)
        for k in range(4):
            z = wide(rows[pl.ds(base + 20 + k, 1), :])
            radius = jnp.abs(cell_z - z)
            rest = jnp.maximum(2.0 - radius, 0.0)
            along_z = jnp.where(
                radius < 1.0,
                1.0 + radius * radius * (1.5 * radius - 2.5),
                0.5 * rest * rest * (1.0 - radius),
            )
            yz = [wide(weights[b][4 + k : 5 + k]) * along_z for b in range(4)]
            xs = [wide(weights[a][k : k + 1]) for a in range(4)]
            table = jnp.concatenate([xs[a] * yz[b] for a in range(4) for b in range(4)], axis=0)
            vortex = [rows[pl.ds(base + 8 + 4 * j + k, 1), :] for j in range(3)]
            slot = slots[0, k]
            work(s, k, slot >> 4, slot & 15, vortex, *split(table))

    def per_group(q, carry):
        base = pl.multiple_of(q * (25 * GROUP), 8)
        for u in range(GROUP):
            per_source(q * GROUP + u, base + 25 * u)
        return carry

    lax.fori_loop(first, last, per_group, 0)


def sampled_row(grads, column, level, vortex, high, low):
    grad = jnp.concatenate(
        [grads[pl.ds(column * 144 + j * 48 + level, 8, stride=16), :] for j in range(3)],
        axis=0,
    )
    left = jnp.concatenate(split(grad), axis=0)
    left = jnp.concatenate([left, left], axis=1)
    value = jnp.dot(left, jnp.concatenate([high, low], axis=0), preferred_element_type=F32)
    value = value[:24] + value[24:]
    stretch = (
        value[0:8] * wide(vortex[0])
        + value[8:16] * wide(vortex[1])
        + value[16:24] * wide(vortex[2])
    )
    return stretch[:3]


def add_patch(mesh, column, level, vortex, high, low):
    v = jnp.concatenate(vortex + [jnp.zeros((5, 128), F32)], axis=0)
    left = jnp.concatenate(split(v), axis=0)
    left = jnp.concatenate([left, left], axis=1)
    patch = lax.dot_general(
        left,
        jnp.concatenate([high, low], axis=1),
        (((1,), (1,)), ((), ())),
        preferred_element_type=F32,
    )
    patch = patch[:3] + patch[8:11]
    at = pl.ds(column * 48 + level, 3, stride=16)
    mesh[at, :] = mesh[at, :] + patch


def sample_kernel(rows, grads, back, mesh, rows_here, grads_here, back_here, mesh_here, sems):
    ahead = EARLY * GROUP * 25
    parts = (pl.ds(0, ahead), pl.ds(ahead, 3200 - ahead))
    fetches = [
        pltpu.make_async_copy(rows.at[part, :], rows_here.at[part, :], sems.at[n])
        for n, part in enumerate(parts)
    ]
    fetches.append(pltpu.make_async_copy(grads, grads_here, sems.at[2]))
    for copy in fetches:
        copy.start()

    def clear(i, carry):
        mesh_here[pl.ds(pl.multiple_of(i * 64, 64), 64), :] = jnp.zeros((64, 128), F32)
        return carry

    lax.fori_loop(0, 48, clear, 0)
    fetches[0].wait()
    each_row(rows_here, lambda s, k, *row: add_patch(mesh_here, *row), 0, EARLY)
    stores = [pltpu.make_async_copy(mesh_here, mesh, sems.at[3])]
    stores[0].start()
    for copy in fetches[1:]:
        copy.wait()

    def work(s, k, *row):
        back_here[pl.ds(s * 12 + k, 3, stride=4), :] = sampled_row(grads_here, *row)

    for n in range(2):
        each_row(rows_here, work, n * 64 // GROUP, (n + 1) * 64 // GROUP)
        half = pl.ds(768 * n, 768)
        stores.append(pltpu.make_async_copy(back_here.at[half, :], back.at[half, :], sems.at[4 + n]))
        stores[-1].start()
    for copy in stores:
        copy.wait()


def sample(rows, grads):
    return pl.pallas_call(
        sample_kernel,
        out_shape=[sds((1536, 128)), sds((3072, 128))],
        in_specs=[ANY] * 2,
        out_specs=[ANY] * 2,
        scratch_shapes=[
            pltpu.VMEM((3200, 128), F32),
            pltpu.VMEM((GRAD_ROWS + GRAD_PAD, 128), F32),
            pltpu.VMEM((1536, 128), F32),
            pltpu.VMEM((3072, 128), F32),
            pltpu.SemaphoreType.DMA((6,)),
        ],
        compiler_params=LARGE,
        cost_estimate=cost(300_000_000, 9_000_000),
        name="sample",
    )(rows, grads)


def deposit_kernel(rows, before, mesh, rows_here, sems):
    ahead = EARLY * GROUP * 25
    part = pl.ds(ahead, 3200 - ahead)
    fetches = [
        pltpu.make_async_copy(rows.at[part, :], rows_here.at[part, :], sems.at[0]),
        pltpu.make_async_copy(before, mesh, sems.at[1]),
    ]
    for copy in fetches:
        copy.start()
    for copy in fetches:
        copy.wait()
    each_row(rows_here, lambda s, k, *row: add_patch(mesh, *row), EARLY, 128 // GROUP)


def deposit(rows, before):
    return pl.pallas_call(
        deposit_kernel,
        out_shape=sds((3072, 128)),
        in_specs=[ANY] * 2,
        out_specs=VMEM,
        scratch_shapes=[pltpu.VMEM((3200, 128), F32), pltpu.SemaphoreType.DMA((2,))],
        compiler_params=LARGE,
        cost_estimate=cost(300_000_000, 40_000_000),
        name="deposit",
    )(rows, before)


def unpack_kernel(places, back, out, turned):
    def move(r, carry):
        place = places[r]
        base = (place >> 2) * 12 + (place & 3)
        turned[pl.ds(r, 3, stride=256), :] = back[pl.ds(base, 3, stride=4), :]
        return carry

    lax.fori_loop(0, 256, move, 0, unroll=8)
    for h in range(2):
        for i in range(3):
            at = i * 256 + h * 128
            out[h, i] = turned[at : at + 128, :].T


def unpack(places, back):
    return pl.pallas_call(
        unpack_kernel,
        out_shape=sds((2, 3, 128, 128)),
        in_specs=[SMEM, VMEM],
        out_specs=VMEM,
        scratch_shapes=[pltpu.VMEM((768, 128), F32)],
        compiler_params=PARAMS,
        cost_estimate=cost(1_000_000, 2_000_000),
        name="unpack",
    )(places, back)


def stepped(value, axis, step):
    count = lax.axis_size(axis)
    first, last = (max(0, -step), min(count, count - step))
    return lax.ppermute(value, axis, [(source, source + step) for source in range(first, last)])


def exchange(value):
    return lax.all_to_all(value, AXES, split_axis=0, concat_axis=0, tiled=True)


def on_device(vorticity, position, counts, owner_ids, slot_ids, velocity):
    slots = slot_ids.reshape(2, 128)
    vel = jnp.transpose(velocity, (0, 1, 3, 2, 4)).reshape(3072, 128)
    leaving = depart(vorticity, position, counts, vel)
    arrivals = [
        stepped(leaving[0], "gx", 1),
        stepped(leaving[1], "gx", -1),
        stepped(leaving[2], "gz", 1),
        stepped(leaving[3], "gz", -1),
    ]
    places, kept = keep(owner_ids[:, 0], vorticity, position, counts, slots)
    ship = route(places, slots, arrivals, kept)
    rows = exchange(ship.reshape(128, 25, 1, 128)).reshape(3200, 128)

    grads = gradient(vel, *arrivals)

    back, mesh = sample(rows, grads)
    back = exchange(back.reshape(128, 3, 4, 128)).reshape(1536, 128)
    mesh = deposit(rows, mesh)
    stretching = unpack(places, back)
    mesh = jnp.transpose(mesh.reshape(4, 16, 3, 16, 128), (0, 1, 3, 2, 4))
    return mesh, stretching


def solution(mesh):
    placed = (
        P(None, None, AXES),
        P(None, None, AXES),
        P(None, AXES),
        P(AXES, None),
        P(AXES),
        P("gx", None, "gz", None, None),
    )
    return jax.shard_map(
        on_device,
        mesh=mesh,
        in_specs=placed,
        out_specs=(P("gx", None, "gz", None, None), P(None, None, None, AXES)),
        check_vma=False,
    )
```

```python
import jax
import jax.numpy as jnp
import numpy as np
from jax import lax
from jax.experimental import pallas as pl
from jax.experimental.pallas import tpu as pltpu
from jax.sharding import PartitionSpec as P

AXES = ("gx", "gz")
F32 = jnp.float32
BF16 = jnp.bfloat16
VMEM = pl.BlockSpec(memory_space=pltpu.VMEM)
SMEM = pl.BlockSpec(memory_space=pltpu.SMEM)
ANY = pl.BlockSpec(memory_space=pl.ANY)
PARAMS = pltpu.CompilerParams(vmem_limit_bytes=16 * 1024 * 1024)
LARGE = pltpu.CompilerParams(vmem_limit_bytes=60 * 1024 * 1024)
GRAD_ROWS = 64 * 9 * 16
GRAD_PAD = 128
GROUP = 16
EARLY = 1


def sds(shape, dtype=F32):
    return jax.ShapeDtypeStruct(shape, dtype)


def cost(flops, read):
    return pl.CostEstimate(flops=flops, bytes_accessed=read, transcendentals=0)


def depart_kernel(vort, pos, counts, vel, d0, d1, d2, d3, v_here, p_here, c_here, u_here, out, sems):
    layer = pl.ds(192, 768)
    fetches = [
        pltpu.make_async_copy(source, target, sems.at[n])
        for n, (source, target) in enumerate(
            ((counts, c_here), (vort, v_here), (pos, p_here), (vel, u_here))
        )
    ]
    sides = [
        pltpu.make_async_copy(u_here.at[pl.ds(3 * 768, 768), :], d0.at[layer, :], sems.at[4]),
        pltpu.make_async_copy(u_here.at[pl.ds(0, 768), :], d1.at[layer, :], sems.at[5]),
    ]
    for copy in fetches:
        copy.start()
    for copy in fetches[:3]:
        copy.wait()
    place = lax.broadcasted_iota(jnp.int32, (32, 128), 0)
    sends = []
    for heading in range(4):
        leaves = place < c_here[heading : heading + 1, :]
        rows = slice(heading * 32, heading * 32 + 32)
        for i in range(3):
            out[heading, 32 * i : 32 * i + 32, :] = jnp.where(leaves, v_here[i, rows, :], 0.0)
            out[heading, 96 + 32 * i : 128 + 32 * i, :] = jnp.where(leaves, p_here[i, rows, :], 0.0)
        if heading < 2:
            target = (d0, d1)[heading].at[pl.ds(0, 192), :]
            sends.append(
                pltpu.make_async_copy(
                    out.at[heading, pl.ds(0, 192), :], target, sems.at[6 + heading]
                )
            )
            sends[-1].start()
    fetches[3].wait()
    for copy in sides:
        copy.start()
    for heading, level in ((2, 15), (3, 0)):
        out[heading, 192:384, :] = u_here[pl.ds(level, 192, stride=16), :]
        target = (d2, d3)[heading - 2]
        sends.append(pltpu.make_async_copy(out.at[heading], target, sems.at[6 + heading]))
        sends[-1].start()
    for copy in sides + sends:
        copy.wait()


def depart(vort, pos, counts, vel):
    return pl.pallas_call(
        depart_kernel,
        out_shape=[sds((960, 128))] * 2 + [sds((384, 128))] * 2,
        in_specs=[ANY] * 4,
        out_specs=[ANY] * 4,
        scratch_shapes=[
            pltpu.VMEM((3, 128, 128), F32),
            pltpu.VMEM((3, 128, 128), F32),
            pltpu.VMEM((4, 128), jnp.int32),
            pltpu.VMEM((3072, 128), F32),
            pltpu.VMEM((4, 384, 128), F32),
            pltpu.SemaphoreType.DMA((10,)),
        ],
        compiler_params=LARGE,
        cost_estimate=cost(400_000, 3_000_000),
        name="depart",
    )(vort, pos, counts, vel)


ORDER = (3, 4, 0, 1, 2, 5)


def send_rows(places, turned, ship, first):
    def move(r, carry):
        place = places[first + r]
        base = (place >> 2) * 25 + (place & 3)
        ship[pl.ds(base, 6, stride=4), :] = turned[pl.ds(r, 6, stride=128), :]
        return carry

    lax.fori_loop(0, 128, move, 0, unroll=8)


def keep_kernel(
    owners, slots, vort, pos, counts, places, marks, turned, tally, v_here, p_here, c_here, sems
):
    fetches = [
        pltpu.make_async_copy(source, target, sems.at[n])
        for n, (source, target) in enumerate(
            ((counts, c_here), (vort, v_here), (pos, p_here))
        )
    ]
    for copy in fetches:
        copy.start()
    marks[...] = jnp.zeros((128, 128), F32)
    lane = lax.broadcasted_iota(jnp.int32, (1, 128), 1)
    for i in range(128):
        tally[i] = 0

    def rank_of(r, carry):
        owner = owners[r]
        rank = tally[owner]
        tally[owner] = rank + 1
        places[r] = owner * 4 + rank
        row = pl.ds(owner, 1)
        marks[row, :] = jnp.where(lane == rank, slots[r].astype(F32), marks[row, :])
        return carry

    lax.fori_loop(0, 256, rank_of, 0, unroll=8)
    for copy in fetches:
        copy.wait()
    place = lax.broadcasted_iota(jnp.int32, (32, 128), 0)
    leaves = [place < c_here[heading : heading + 1, :] for heading in range(4)]
    for at, comp in enumerate(ORDER):
        if comp < 3:
            kept = jnp.concatenate(
                [
                    jnp.where(leaves[h], 0.0, v_here[comp, 32 * h : 32 * h + 32, :])
                    for h in range(4)
                ],
                axis=0,
            )
        else:
            kept = p_here[comp - 3]
        turned[at * 128 : at * 128 + 128, :] = kept.T


def keep(owners, slots, vort, pos, counts):
    return pl.pallas_call(
        keep_kernel,
        out_shape=[sds((256,), jnp.int32), sds((128, 128)), sds((768, 128))],
        in_specs=[SMEM] * 2 + [ANY] * 3,
        out_specs=[SMEM, VMEM, VMEM],
        scratch_shapes=[
            pltpu.SMEM((128,), jnp.int32),
            pltpu.VMEM((3, 128, 128), F32),
            pltpu.VMEM((3, 128, 128), F32),
            pltpu.VMEM((4, 128), jnp.int32),
            pltpu.SemaphoreType.DMA((3,)),
        ],
        compiler_params=LARGE,
        cost_estimate=cost(1_000_000, 4_000_000),
        name="keep",
    )(owners, slots, vort, pos, counts)


def route_kernel(
    places, marks, a0, a1, a2, a3, kept, ship, turned, kept_here, came_here, m_here, sems
):
    fetches = [
        pltpu.make_async_copy(source.at[pl.ds(0, 192), :], came_here.at[n], sems.at[n])
        for n, source in enumerate((a0, a1, a2, a3))
    ]
    fetches.append(pltpu.make_async_copy(marks, m_here, sems.at[4]))
    fetches.append(pltpu.make_async_copy(kept, kept_here, sems.at[5]))
    for copy in fetches:
        copy.start()

    def clear(i, carry):
        ship[pl.ds(pl.multiple_of(i * 64, 64), 64), :] = jnp.zeros((64, 128), F32)
        return carry

    lax.fori_loop(0, 50, clear, 0)
    fetches[5].wait()
    send_rows(places, kept_here, ship, 0)
    for copy in fetches[:5]:
        copy.wait()
    for at, comp in enumerate(ORDER):
        came = jnp.concatenate(
            [came_here[n, 32 * comp : 32 * comp + 32, :] for n in range(4)], axis=0
        )
        turned[at * 128 : at * 128 + 128, :] = came.T
    send_rows(places, turned, ship, 128)
    ship[pl.ds(24, 128, stride=25), :] = m_here[...]


def route(places, marks, arrivals, kept):
    return pl.pallas_call(
        route_kernel,
        out_shape=sds((3200, 128)),
        in_specs=[SMEM] + [ANY] * 6,
        out_specs=VMEM,
        scratch_shapes=[
            pltpu.VMEM((768, 128), F32),
            pltpu.VMEM((768, 128), F32),
            pltpu.VMEM((4, 192, 128), F32),
            pltpu.VMEM((128, 128), F32),
            pltpu.SemaphoreType.DMA((6,)),
        ],
        compiler_params=LARGE,
        cost_estimate=cost(1_000_000, 4_000_000),
        name="route",
    )(places, marks, *arrivals, kept)


def stencil(stride, per):
    here, before, after = (np.zeros((128, 128), np.float32) for _ in range(3))
    factors = {1: 45.0, -1: -45.0, 2: -9.0, -2: 9.0, 3: 1.0, -3: -1.0}
    for lane in range(128):
        digit = lane // stride % per
        for offset, factor in factors.items():
            at = lane + offset * stride
            if digit + offset >= per:
                after[at - per * stride, lane] = factor
            elif digit + offset < 0:
                before[at + per * stride, lane] = factor
            else:
                here[at, lane] = factor
    return here, before, after


def matrices():
    along_x = np.concatenate(stencil(32, 4) * 2)
    along_y = np.concatenate(stencil(8, 4) * 2)
    here, before, after = stencil(1, 8)
    along_z = np.concatenate((here, before + after) * 2)
    return [jnp.asarray(m, BF16) for m in (along_x, along_y, along_z)]


def split(value):
    high = value.astype(BF16)
    return high, (value - high.astype(F32)).astype(BF16)


def gradient_kernel(vel, xb, xa, zb, za, mx, my, mz, out, high, low, z_high, z_low):
    late = lax.broadcasted_iota(jnp.int32, (16, 128), 1) % 8 >= 5

    def put(sx, sy, value):
        at = pl.ds(pl.multiple_of((sx * 18 + sy) * 48, 16), 48)
        high[at, :], low[at, :] = split(value)

    def fill(sy, carry):
        rows = pl.ds(pl.multiple_of(192 + sy * 48, 16), 48)
        put(0, sy + 1, xb[rows, :])
        put(5, sy + 1, xa[rows, :])
        for sx in range(4):
            row = (sx * 16 + sy) * 48
            value = vel[pl.ds(pl.multiple_of(row, 16), 48), :]
            put(sx + 1, sy + 1, value)
            for i in range(3):
                c = value[16 * i : 16 * i + 16]
                edge = pl.ds(192 + (sx * 16 + sy) * 3 + i, 1)
                before = jnp.concatenate([zb[edge, :], c[:15]], axis=0)
                after = jnp.concatenate([c[1:], za[edge, :]], axis=0)
                at = pl.ds(pl.multiple_of(row + 16 * i, 16), 16)
                z_high[at, :], z_low[at, :] = split(jnp.where(late, before, after))
        return carry

    lax.fori_loop(0, 16, fill, 0)
    for sx in range(4):
        put(sx + 1, 0, vel[(sx * 16 + 15) * 48 : (sx * 16 + 16) * 48, :])
        put(sx + 1, 17, vel[sx * 16 * 48 : (sx * 16 + 1) * 48, :])

    def per_x(sx, carry):
        def part(ref, dx, dy):
            at = pl.multiple_of(((sx + 1 + dx) * 18 + 1 + dy) * 48, 16)
            return ref[pl.ds(at, 768), :]

        both = (high, low)
        own = pl.ds(pl.multiple_of(sx * 768, 16), 768)
        along_x = [part(ref, dx, 0) for ref in both for dx in (0, -1, 1)]
        along_y = [part(ref, 0, dy) for ref in both for dy in (0, -1, 1)]
        along_z = [part(high, 0, 0), z_high[own, :], part(low, 0, 0), z_low[own, :]]
        for j, (parts, matrix) in enumerate(((along_x, mx), (along_y, my), (along_z, mz))):
            value = jnp.dot(
                jnp.concatenate(parts, axis=1), matrix[...], preferred_element_type=F32
            ) * (1.0 / 60.0)
            for sy in range(16):
                at = pl.multiple_of(((sx * 16 + sy) * 9 + 3 * j) * 16, 16)
                out[pl.ds(at, 48), :] = value[48 * sy : 48 * sy + 48]
        return carry

    lax.fori_loop(0, 4, per_x, 0)
    out[GRAD_ROWS:, :] = jnp.zeros((GRAD_PAD, 128), F32)


def gradient(vel, xb, xa, zb, za):
    return pl.pallas_call(
        gradient_kernel,
        out_shape=sds((GRAD_ROWS + GRAD_PAD, 128)),
        in_specs=[VMEM] * 8,
        out_specs=VMEM,
        scratch_shapes=[pltpu.VMEM((6 * 18 * 48, 128), BF16)] * 2
        + [pltpu.VMEM((3072, 128), BF16)] * 2,
        compiler_params=PARAMS,
        cost_estimate=cost(20_000_000, 8_000_000),
        name="gradient",
    )(vel, xb, xa, zb, za, *matrices())


def wide(row):
    return jnp.broadcast_to(row, (8, 128))


def each_row(rows, work, first, last):
    cell_z = lax.broadcasted_iota(jnp.int32, (8, 128), 0).astype(F32)

    def per_source(s, base):
        f = rows[pl.ds(base, 8), :] - 1.0
        g = 1.0 - f
        weights = (
            -0.5 * f * g * g,
            1.0 + f * f * (1.5 * f - 2.5),
            1.0 + g * g * (1.5 * g - 2.5),
            -0.5 * g * f * f,
        )
        slots = rows[pl.ds(base + 24, 1), :].astype(jnp.int32)
        for k in range(4):
            z = wide(rows[pl.ds(base + 20 + k, 1), :])
            radius = jnp.abs(cell_z - z)
            rest = jnp.maximum(2.0 - radius, 0.0)
            along_z = jnp.where(
                radius < 1.0,
                1.0 + radius * radius * (1.5 * radius - 2.5),
                0.5 * rest * rest * (1.0 - radius),
            )
            yz = [wide(weights[b][4 + k : 5 + k]) * along_z for b in range(4)]
            xs = [wide(weights[a][k : k + 1]) for a in range(4)]
            vortex = [rows[pl.ds(base + 8 + 4 * j + k, 1), :] for j in range(3)]
            slot = slots[0, k]
            work(s, k, slot >> 4, slot & 15, vortex, xs, yz)

    def per_group(q, carry):
        base = pl.multiple_of(q * (25 * GROUP), 8)
        for u in range(GROUP):
            per_source(q * GROUP + u, base + 25 * u)
        return carry

    lax.fori_loop(first, last, per_group, 0)


def weight_table(xs, yz):
    return split(jnp.concatenate([xs[a] * yz[b] for a in range(4) for b in range(4)], axis=0))


def sampled_row(grads, column, level, vortex, xs, yz):
    high, low = weight_table(xs, yz)
    grad = jnp.concatenate(
        [grads[pl.ds(column * 144 + j * 48 + level, 8, stride=16), :] for j in range(3)],
        axis=0,
    )
    left = jnp.concatenate(split(grad), axis=0)
    left = jnp.concatenate([left, left], axis=1)
    value = jnp.dot(left, jnp.concatenate([high, low], axis=0), preferred_element_type=F32)
    value = value[:24] + value[24:]
    stretch = (
        value[0:8] * wide(vortex[0])
        + value[8:16] * wide(vortex[1])
        + value[16:24] * wide(vortex[2])
    )
    return stretch[:3]


def add_patch(mesh, column, level, vortex, xs, yz):
    high, low = weight_table(xs, yz)
    v = jnp.concatenate(vortex + [jnp.zeros((5, 128), F32)], axis=0)
    left = jnp.concatenate(split(v), axis=0)
    left = jnp.concatenate([left, left], axis=1)
    patch = lax.dot_general(
        left,
        jnp.concatenate([high, low], axis=1),
        (((1,), (1,)), ((), ())),
        preferred_element_type=F32,
    )
    patch = patch[:3] + patch[8:11]
    at = pl.ds(column * 48 + level, 3, stride=16)
    mesh[at, :] = mesh[at, :] + patch


def sample_kernel(rows, grads, back, mesh, rows_here, grads_here, back_here, mesh_here, sems):
    ahead = EARLY * GROUP * 25
    parts = (pl.ds(0, ahead), pl.ds(ahead, 3200 - ahead))
    fetches = [
        pltpu.make_async_copy(rows.at[part, :], rows_here.at[part, :], sems.at[n])
        for n, part in enumerate(parts)
    ]
    fetches.append(pltpu.make_async_copy(grads, grads_here, sems.at[2]))
    for copy in fetches:
        copy.start()

    def clear(i, carry):
        mesh_here[pl.ds(pl.multiple_of(i * 64, 64), 64), :] = jnp.zeros((64, 128), F32)
        return carry

    lax.fori_loop(0, 48, clear, 0)
    fetches[0].wait()
    each_row(rows_here, lambda s, k, *row: add_patch(mesh_here, *row), 0, EARLY)
    stores = [pltpu.make_async_copy(mesh_here, mesh, sems.at[3])]
    stores[0].start()
    for copy in fetches[1:]:
        copy.wait()

    def work(s, k, *row):
        back_here[pl.ds(s * 12 + k, 3, stride=4), :] = sampled_row(grads_here, *row)

    for n in range(2):
        each_row(rows_here, work, n * 64 // GROUP, (n + 1) * 64 // GROUP)
        half = pl.ds(768 * n, 768)
        stores.append(pltpu.make_async_copy(back_here.at[half, :], back.at[half, :], sems.at[4 + n]))
        stores[-1].start()
    for copy in stores:
        copy.wait()


def sample(rows, grads):
    return pl.pallas_call(
        sample_kernel,
        out_shape=[sds((1536, 128)), sds((3072, 128))],
        in_specs=[ANY] * 2,
        out_specs=[ANY] * 2,
        scratch_shapes=[
            pltpu.VMEM((3200, 128), F32),
            pltpu.VMEM((GRAD_ROWS + GRAD_PAD, 128), F32),
            pltpu.VMEM((1536, 128), F32),
            pltpu.VMEM((3072, 128), F32),
            pltpu.SemaphoreType.DMA((6,)),
        ],
        compiler_params=LARGE,
        cost_estimate=cost(300_000_000, 9_000_000),
        name="sample",
    )(rows, grads)


def deposit_kernel(rows, before, mesh, rows_here, sems):
    ahead = EARLY * GROUP * 25
    part = pl.ds(ahead, 3200 - ahead)
    fetches = [
        pltpu.make_async_copy(rows.at[part, :], rows_here.at[part, :], sems.at[0]),
        pltpu.make_async_copy(before, mesh, sems.at[1]),
    ]
    for copy in fetches:
        copy.start()
    for copy in fetches:
        copy.wait()
    each_row(rows_here, lambda s, k, *row: add_patch(mesh, *row), EARLY, 128 // GROUP)


def deposit(rows, before):
    return pl.pallas_call(
        deposit_kernel,
        out_shape=sds((3072, 128)),
        in_specs=[ANY] * 2,
        out_specs=VMEM,
        scratch_shapes=[pltpu.VMEM((3200, 128), F32), pltpu.SemaphoreType.DMA((2,))],
        compiler_params=LARGE,
        cost_estimate=cost(300_000_000, 40_000_000),
        name="deposit",
    )(rows, before)


def unpack_kernel(places, back, out, turned):
    def move(r, carry):
        place = places[r]
        base = (place >> 2) * 12 + (place & 3)
        turned[pl.ds(r, 3, stride=256), :] = back[pl.ds(base, 3, stride=4), :]
        return carry

    lax.fori_loop(0, 256, move, 0, unroll=8)
    for h in range(2):
        for i in range(3):
            at = i * 256 + h * 128
            out[h, i] = turned[at : at + 128, :].T


def unpack(places, back):
    return pl.pallas_call(
        unpack_kernel,
        out_shape=sds((2, 3, 128, 128)),
        in_specs=[SMEM, VMEM],
        out_specs=VMEM,
        scratch_shapes=[pltpu.VMEM((768, 128), F32)],
        compiler_params=PARAMS,
        cost_estimate=cost(1_000_000, 2_000_000),
        name="unpack",
    )(places, back)


def stepped(value, axis, step):
    count = lax.axis_size(axis)
    first, last = (max(0, -step), min(count, count - step))
    return lax.ppermute(value, axis, [(source, source + step) for source in range(first, last)])


def exchange(value):
    return lax.all_to_all(value, AXES, split_axis=0, concat_axis=0, tiled=True)


def on_device(vorticity, position, counts, owner_ids, slot_ids, velocity):
    vel = jnp.transpose(velocity, (0, 1, 3, 2, 4)).reshape(3072, 128)
    leaving = depart(vorticity, position, counts, vel)
    arrivals = [
        stepped(leaving[0], "gx", 1),
        stepped(leaving[1], "gx", -1),
        stepped(leaving[2], "gz", 1),
        stepped(leaving[3], "gz", -1),
    ]
    places, marks, kept = keep(owner_ids[:, 0], slot_ids, vorticity, position, counts)
    ship = route(places, marks, arrivals, kept)
    rows = exchange(ship.reshape(128, 25, 1, 128)).reshape(3200, 128)

    grads = gradient(vel, *arrivals)

    back, mesh = sample(rows, grads)
    back = exchange(back.reshape(128, 3, 4, 128)).reshape(1536, 128)
    mesh = deposit(rows, mesh)
    stretching = unpack(places, back)
    mesh = jnp.transpose(mesh.reshape(4, 16, 3, 16, 128), (0, 1, 3, 2, 4))
    return mesh, stretching


def solution(mesh):
    placed = (
        P(None, None, AXES),
        P(None, None, AXES),
        P(None, AXES),
        P(AXES, None),
        P(AXES),
        P("gx", None, "gz", None, None),
    )
    return jax.shard_map(
        on_device,
        mesh=mesh,
        in_specs=placed,
        out_specs=(P("gx", None, "gz", None, None), P(None, None, None, AXES)),
        check_vma=False,
    )
```

```python
import jax
import jax.numpy as jnp
import numpy as np
from jax import lax
from jax.experimental import pallas as pl
from jax.experimental.pallas import tpu as pltpu
from jax.sharding import PartitionSpec as P

AXES = ("gx", "gz")
F32 = jnp.float32
BF16 = jnp.bfloat16
VMEM = pl.BlockSpec(memory_space=pltpu.VMEM)
SMEM = pl.BlockSpec(memory_space=pltpu.SMEM)
ANY = pl.BlockSpec(memory_space=pl.ANY)
PARAMS = pltpu.CompilerParams(vmem_limit_bytes=16 * 1024 * 1024)
LARGE = pltpu.CompilerParams(vmem_limit_bytes=60 * 1024 * 1024)
GRAD_ROWS = 64 * 9 * 16
GRAD_PAD = 128
GROUP = 16
EARLY = 1


def sds(shape, dtype=F32):
    return jax.ShapeDtypeStruct(shape, dtype)


def cost(flops, read):
    return pl.CostEstimate(flops=flops, bytes_accessed=read, transcendentals=0)


def depart_kernel(vort, pos, counts, vel, d0, d1, d2, d3, v_here, p_here, c_here, u_here, out, sems):
    layer = pl.ds(192, 768)
    fetches = [
        pltpu.make_async_copy(source, target, sems.at[n])
        for n, (source, target) in enumerate(
            ((counts, c_here), (vort, v_here), (pos, p_here), (vel, u_here))
        )
    ]
    sides = [
        pltpu.make_async_copy(u_here.at[pl.ds(3 * 768, 768), :], d0.at[layer, :], sems.at[4]),
        pltpu.make_async_copy(u_here.at[pl.ds(0, 768), :], d1.at[layer, :], sems.at[5]),
    ]
    for copy in fetches:
        copy.start()
    for copy in fetches[:3]:
        copy.wait()
    place = lax.broadcasted_iota(jnp.int32, (32, 128), 0)
    sends = []
    for heading in range(4):
        leaves = place < c_here[heading : heading + 1, :]
        rows = slice(heading * 32, heading * 32 + 32)
        for i in range(3):
            out[heading, 32 * i : 32 * i + 32, :] = jnp.where(leaves, v_here[i, rows, :], 0.0)
            out[heading, 96 + 32 * i : 128 + 32 * i, :] = jnp.where(leaves, p_here[i, rows, :], 0.0)
        if heading < 2:
            target = (d0, d1)[heading].at[pl.ds(0, 192), :]
            sends.append(
                pltpu.make_async_copy(
                    out.at[heading, pl.ds(0, 192), :], target, sems.at[6 + heading]
                )
            )
            sends[-1].start()
    fetches[3].wait()
    for copy in sides:
        copy.start()
    for heading, level in ((2, 15), (3, 0)):
        out[heading, 192:384, :] = u_here[pl.ds(level, 192, stride=16), :]
        target = (d2, d3)[heading - 2]
        sends.append(pltpu.make_async_copy(out.at[heading], target, sems.at[6 + heading]))
        sends[-1].start()
    for copy in sides + sends:
        copy.wait()


def depart(vort, pos, counts, vel):
    return pl.pallas_call(
        depart_kernel,
        out_shape=[sds((960, 128))] * 2 + [sds((384, 128))] * 2,
        in_specs=[ANY] * 4,
        out_specs=[ANY] * 4,
        scratch_shapes=[
            pltpu.VMEM((3, 128, 128), F32),
            pltpu.VMEM((3, 128, 128), F32),
            pltpu.VMEM((4, 128), jnp.int32),
            pltpu.VMEM((3072, 128), F32),
            pltpu.VMEM((4, 384, 128), F32),
            pltpu.SemaphoreType.DMA((10,)),
        ],
        compiler_params=LARGE,
        cost_estimate=cost(400_000, 3_000_000),
        name="depart",
    )(vort, pos, counts, vel)


ORDER = (3, 4, 0, 1, 2, 5)


def send_rows(places, turned, ship, first):
    def move(r, carry):
        place = places[first + r]
        base = (place >> 2) * 25 + (place & 3)
        ship[pl.ds(base, 6, stride=4), :] = turned[pl.ds(r, 6, stride=128), :]
        return carry

    lax.fori_loop(0, 128, move, 0, unroll=8)


def keep_kernel(
    owners, slots, vort, pos, counts, places, marks, turned, tally, v_here, p_here, c_here, sems
):
    fetches = [
        pltpu.make_async_copy(source, target, sems.at[n])
        for n, (source, target) in enumerate(
            ((counts, c_here), (vort, v_here), (pos, p_here))
        )
    ]
    for copy in fetches:
        copy.start()
    marks[...] = jnp.zeros((128, 128), F32)
    lane = lax.broadcasted_iota(jnp.int32, (1, 128), 1)
    for i in range(128):
        tally[i] = 0

    def rank_of(r, carry):
        owner = owners[r]
        rank = tally[owner]
        tally[owner] = rank + 1
        places[r] = owner * 4 + rank
        row = pl.ds(owner, 1)
        marks[row, :] = jnp.where(lane == rank, slots[r].astype(F32), marks[row, :])
        return carry

    lax.fori_loop(0, 256, rank_of, 0, unroll=8)
    for copy in fetches:
        copy.wait()
    place = lax.broadcasted_iota(jnp.int32, (32, 128), 0)
    leaves = [place < c_here[heading : heading + 1, :] for heading in range(4)]
    for at, comp in enumerate(ORDER):
        if comp < 3:
            kept = jnp.concatenate(
                [
                    jnp.where(leaves[h], 0.0, v_here[comp, 32 * h : 32 * h + 32, :])
                    for h in range(4)
                ],
                axis=0,
            )
        else:
            kept = p_here[comp - 3]
        turned[at * 128 : at * 128 + 128, :] = kept.T


def keep(owners, slots, vort, pos, counts):
    return pl.pallas_call(
        keep_kernel,
        out_shape=[sds((256,), jnp.int32), sds((128, 128)), sds((768, 128))],
        in_specs=[SMEM] * 2 + [ANY] * 3,
        out_specs=[SMEM, VMEM, VMEM],
        scratch_shapes=[
            pltpu.SMEM((128,), jnp.int32),
            pltpu.VMEM((3, 128, 128), F32),
            pltpu.VMEM((3, 128, 128), F32),
            pltpu.VMEM((4, 128), jnp.int32),
            pltpu.SemaphoreType.DMA((3,)),
        ],
        compiler_params=LARGE,
        cost_estimate=cost(1_000_000, 4_000_000),
        name="keep",
    )(owners, slots, vort, pos, counts)


def route_kernel(
    places,
    marks,
    a0,
    a1,
    a2,
    a3,
    kept,
    ship,
    turned,
    kept_here,
    came_here,
    m_here,
    places_here,
    sems,
):
    fetches = [
        pltpu.make_async_copy(source.at[pl.ds(0, 192), :], came_here.at[n], sems.at[n])
        for n, source in enumerate((a0, a1, a2, a3))
    ]
    fetches.append(pltpu.make_async_copy(marks, m_here, sems.at[4]))
    fetches.append(pltpu.make_async_copy(kept, kept_here, sems.at[5]))
    fetches.append(pltpu.make_async_copy(places, places_here, sems.at[6]))
    for copy in fetches:
        copy.start()

    def clear(i, carry):
        ship[pl.ds(pl.multiple_of(i * 64, 64), 64), :] = jnp.zeros((64, 128), F32)
        return carry

    lax.fori_loop(0, 50, clear, 0)
    for copy in fetches[5:]:
        copy.wait()
    send_rows(places_here, kept_here, ship, 0)
    for copy in fetches[:5]:
        copy.wait()
    for at, comp in enumerate(ORDER):
        came = jnp.concatenate(
            [came_here[n, 32 * comp : 32 * comp + 32, :] for n in range(4)], axis=0
        )
        turned[at * 128 : at * 128 + 128, :] = came.T
    send_rows(places_here, turned, ship, 128)
    ship[pl.ds(24, 128, stride=25), :] = m_here[...]


def route(places, marks, arrivals, kept):
    return pl.pallas_call(
        route_kernel,
        out_shape=sds((3200, 128)),
        in_specs=[ANY] * 7,
        out_specs=VMEM,
        scratch_shapes=[
            pltpu.VMEM((768, 128), F32),
            pltpu.VMEM((768, 128), F32),
            pltpu.VMEM((4, 192, 128), F32),
            pltpu.VMEM((128, 128), F32),
            pltpu.SMEM((256,), jnp.int32),
            pltpu.SemaphoreType.DMA((7,)),
        ],
        compiler_params=LARGE,
        cost_estimate=cost(1_000_000, 4_000_000),
        name="route",
    )(places, marks, *arrivals, kept)


def stencil(stride, per):
    here, before, after = (np.zeros((128, 128), np.float32) for _ in range(3))
    factors = {1: 45.0, -1: -45.0, 2: -9.0, -2: 9.0, 3: 1.0, -3: -1.0}
    for lane in range(128):
        digit = lane // stride % per
        for offset, factor in factors.items():
            at = lane + offset * stride
            if digit + offset >= per:
                after[at - per * stride, lane] = factor
            elif digit + offset < 0:
                before[at + per * stride, lane] = factor
            else:
                here[at, lane] = factor
    return here, before, after


def matrices():
    along_x = np.concatenate(stencil(32, 4) * 2)
    along_y = np.concatenate(stencil(8, 4) * 2)
    here, before, after = stencil(1, 8)
    along_z = np.concatenate((here, before + after) * 2)
    return [jnp.asarray(m, BF16) for m in (along_x, along_y, along_z)]


def split(value):
    high = value.astype(BF16)
    return high, (value - high.astype(F32)).astype(BF16)


def gradient_kernel(vel, xb, xa, zb, za, mx, my, mz, out, high, low, z_high, z_low):
    late = lax.broadcasted_iota(jnp.int32, (16, 128), 1) % 8 >= 5

    def put(sx, sy, value):
        at = pl.ds(pl.multiple_of((sx * 18 + sy) * 48, 16), 48)
        high[at, :], low[at, :] = split(value)

    def fill(sy, carry):
        rows = pl.ds(pl.multiple_of(192 + sy * 48, 16), 48)
        put(0, sy + 1, xb[rows, :])
        put(5, sy + 1, xa[rows, :])
        for sx in range(4):
            row = (sx * 16 + sy) * 48
            value = vel[pl.ds(pl.multiple_of(row, 16), 48), :]
            put(sx + 1, sy + 1, value)
            for i in range(3):
                c = value[16 * i : 16 * i + 16]
                edge = pl.ds(192 + (sx * 16 + sy) * 3 + i, 1)
                before = jnp.concatenate([zb[edge, :], c[:15]], axis=0)
                after = jnp.concatenate([c[1:], za[edge, :]], axis=0)
                at = pl.ds(pl.multiple_of(row + 16 * i, 16), 16)
                z_high[at, :], z_low[at, :] = split(jnp.where(late, before, after))
        return carry

    lax.fori_loop(0, 16, fill, 0)
    for sx in range(4):
        put(sx + 1, 0, vel[(sx * 16 + 15) * 48 : (sx * 16 + 16) * 48, :])
        put(sx + 1, 17, vel[sx * 16 * 48 : (sx * 16 + 1) * 48, :])

    def per_x(sx, carry):
        def part(ref, dx, dy):
            at = pl.multiple_of(((sx + 1 + dx) * 18 + 1 + dy) * 48, 16)
            return ref[pl.ds(at, 768), :]

        both = (high, low)
        own = pl.ds(pl.multiple_of(sx * 768, 16), 768)
        along_x = [part(ref, dx, 0) for ref in both for dx in (0, -1, 1)]
        along_y = [part(ref, 0, dy) for ref in both for dy in (0, -1, 1)]
        along_z = [part(high, 0, 0), z_high[own, :], part(low, 0, 0), z_low[own, :]]
        for j, (parts, matrix) in enumerate(((along_x, mx), (along_y, my), (along_z, mz))):
            value = jnp.dot(
                jnp.concatenate(parts, axis=1), matrix[...], preferred_element_type=F32
            ) * (1.0 / 60.0)
            for sy in range(16):
                at = pl.multiple_of(((sx * 16 + sy) * 9 + 3 * j) * 16, 16)
                out[pl.ds(at, 48), :] = value[48 * sy : 48 * sy + 48]
        return carry

    lax.fori_loop(0, 4, per_x, 0)
    out[GRAD_ROWS:, :] = jnp.zeros((GRAD_PAD, 128), F32)


def gradient(vel, xb, xa, zb, za):
    return pl.pallas_call(
        gradient_kernel,
        out_shape=sds((GRAD_ROWS + GRAD_PAD, 128)),
        in_specs=[VMEM] * 8,
        out_specs=VMEM,
        scratch_shapes=[pltpu.VMEM((6 * 18 * 48, 128), BF16)] * 2
        + [pltpu.VMEM((3072, 128), BF16)] * 2,
        compiler_params=PARAMS,
        cost_estimate=cost(20_000_000, 8_000_000),
        name="gradient",
    )(vel, xb, xa, zb, za, *matrices())


def wide(row):
    return jnp.broadcast_to(row, (8, 128))


def each_row(rows, work, first, last):
    cell_z = lax.broadcasted_iota(jnp.int32, (8, 128), 0).astype(F32)

    def per_source(s, base):
        f = rows[pl.ds(base, 8), :] - 1.0
        g = 1.0 - f
        weights = (
            -0.5 * f * g * g,
            1.0 + f * f * (1.5 * f - 2.5),
            1.0 + g * g * (1.5 * g - 2.5),
            -0.5 * g * f * f,
        )
        slots = rows[pl.ds(base + 24, 1), :].astype(jnp.int32)
        for k in range(4):
            z = wide(rows[pl.ds(base + 20 + k, 1), :])
            radius = jnp.abs(cell_z - z)
            rest = jnp.maximum(2.0 - radius, 0.0)
            along_z = jnp.where(
                radius < 1.0,
                1.0 + radius * radius * (1.5 * radius - 2.5),
                0.5 * rest * rest * (1.0 - radius),
            )
            yz = [wide(weights[b][4 + k : 5 + k]) * along_z for b in range(4)]
            xs = [wide(weights[a][k : k + 1]) for a in range(4)]
            vortex = [rows[pl.ds(base + 8 + 4 * j + k, 1), :] for j in range(3)]
            slot = slots[0, k]
            work(s, k, slot >> 4, slot & 15, vortex, xs, yz)

    def per_group(q, carry):
        base = pl.multiple_of(q * (25 * GROUP), 8)
        for u in range(GROUP):
            per_source(q * GROUP + u, base + 25 * u)
        return carry

    lax.fori_loop(first, last, per_group, 0)


def weight_table(xs, yz):
    return split(jnp.concatenate([xs[a] * yz[b] for a in range(4) for b in range(4)], axis=0))


def sampled_row(grads, column, level, vortex, xs, yz):
    high, low = weight_table(xs, yz)
    grad = jnp.concatenate(
        [grads[pl.ds(column * 144 + j * 48 + level, 8, stride=16), :] for j in range(3)],
        axis=0,
    )
    left = jnp.concatenate(split(grad), axis=0)
    left = jnp.concatenate([left, left], axis=1)
    value = jnp.dot(left, jnp.concatenate([high, low], axis=0), preferred_element_type=F32)
    value = value[:24] + value[24:]
    stretch = (
        value[0:8] * wide(vortex[0])
        + value[8:16] * wide(vortex[1])
        + value[16:24] * wide(vortex[2])
    )
    return stretch[:3]


def add_patch(mesh, column, level, vortex, xs, yz):
    high, low = weight_table(xs, yz)
    v = jnp.concatenate(vortex + [jnp.zeros((5, 128), F32)], axis=0)
    left = jnp.concatenate(split(v), axis=0)
    left = jnp.concatenate([left, left], axis=1)
    patch = lax.dot_general(
        left,
        jnp.concatenate([high, low], axis=1),
        (((1,), (1,)), ((), ())),
        preferred_element_type=F32,
    )
    patch = patch[:3] + patch[8:11]
    at = pl.ds(column * 48 + level, 3, stride=16)
    mesh[at, :] = mesh[at, :] + patch


def sample_kernel(rows, grads, back, mesh, rows_here, grads_here, back_here, mesh_here, sems):
    ahead = EARLY * GROUP * 25
    parts = (pl.ds(0, ahead), pl.ds(ahead, 3200 - ahead))
    fetches = [
        pltpu.make_async_copy(rows.at[part, :], rows_here.at[part, :], sems.at[n])
        for n, part in enumerate(parts)
    ]
    fetches.append(pltpu.make_async_copy(grads, grads_here, sems.at[2]))
    for copy in fetches:
        copy.start()

    def clear(i, carry):
        mesh_here[pl.ds(pl.multiple_of(i * 64, 64), 64), :] = jnp.zeros((64, 128), F32)
        return carry

    lax.fori_loop(0, 48, clear, 0)
    fetches[0].wait()
    each_row(rows_here, lambda s, k, *row: add_patch(mesh_here, *row), 0, EARLY)
    stores = [pltpu.make_async_copy(mesh_here, mesh, sems.at[3])]
    stores[0].start()
    for copy in fetches[1:]:
        copy.wait()

    def work(s, k, *row):
        back_here[pl.ds(s * 12 + k, 3, stride=4), :] = sampled_row(grads_here, *row)

    for n in range(2):
        each_row(rows_here, work, n * 64 // GROUP, (n + 1) * 64 // GROUP)
        half = pl.ds(768 * n, 768)
        stores.append(pltpu.make_async_copy(back_here.at[half, :], back.at[half, :], sems.at[4 + n]))
        stores[-1].start()
    for copy in stores:
        copy.wait()


def sample(rows, grads):
    return pl.pallas_call(
        sample_kernel,
        out_shape=[sds((1536, 128)), sds((3072, 128))],
        in_specs=[ANY] * 2,
        out_specs=[ANY] * 2,
        scratch_shapes=[
            pltpu.VMEM((3200, 128), F32),
            pltpu.VMEM((GRAD_ROWS + GRAD_PAD, 128), F32),
            pltpu.VMEM((1536, 128), F32),
            pltpu.VMEM((3072, 128), F32),
            pltpu.SemaphoreType.DMA((6,)),
        ],
        compiler_params=LARGE,
        cost_estimate=cost(300_000_000, 9_000_000),
        name="sample",
    )(rows, grads)


def deposit_kernel(rows, before, mesh, rows_here, sems):
    ahead = EARLY * GROUP * 25
    part = pl.ds(ahead, 3200 - ahead)
    fetches = [
        pltpu.make_async_copy(rows.at[part, :], rows_here.at[part, :], sems.at[0]),
        pltpu.make_async_copy(before, mesh, sems.at[1]),
    ]
    for copy in fetches:
        copy.start()
    for copy in fetches:
        copy.wait()
    each_row(rows_here, lambda s, k, *row: add_patch(mesh, *row), EARLY, 128 // GROUP)


def deposit(rows, before):
    return pl.pallas_call(
        deposit_kernel,
        out_shape=sds((3072, 128)),
        in_specs=[ANY] * 2,
        out_specs=VMEM,
        scratch_shapes=[pltpu.VMEM((3200, 128), F32), pltpu.SemaphoreType.DMA((2,))],
        compiler_params=LARGE,
        cost_estimate=cost(300_000_000, 40_000_000),
        name="deposit",
    )(rows, before)


def unpack_kernel(places, back, out, turned, whole, sems):
    def move(r, carry):
        place = places[r]
        base = (place >> 2) * 12 + (place & 3)
        turned[pl.ds(r, 3, stride=256), :] = back[pl.ds(base, 3, stride=4), :]
        return carry

    stores = []
    for h in range(2):
        lax.fori_loop(h * 128, h * 128 + 128, move, 0, unroll=16)
        for i in range(3):
            at = i * 256 + h * 128
            whole[h, i] = turned[at : at + 128, :].T
        stores.append(pltpu.make_async_copy(whole.at[h], out.at[h], sems.at[h]))
        stores[-1].start()
    for copy in stores:
        copy.wait()


def unpack(places, back):
    return pl.pallas_call(
        unpack_kernel,
        out_shape=sds((2, 3, 128, 128)),
        in_specs=[SMEM, VMEM],
        out_specs=ANY,
        scratch_shapes=[
            pltpu.VMEM((768, 128), F32),
            pltpu.VMEM((2, 3, 128, 128), F32),
            pltpu.SemaphoreType.DMA((2,)),
        ],
        compiler_params=PARAMS,
        cost_estimate=cost(1_000_000, 2_000_000),
        name="unpack",
    )(places, back)


def stepped(value, axis, step):
    count = lax.axis_size(axis)
    first, last = (max(0, -step), min(count, count - step))
    return lax.ppermute(value, axis, [(source, source + step) for source in range(first, last)])


def exchange(value):
    return lax.all_to_all(value, AXES, split_axis=0, concat_axis=0, tiled=True)


def on_device(vorticity, position, counts, owner_ids, slot_ids, velocity):
    vel = jnp.transpose(velocity, (0, 1, 3, 2, 4)).reshape(3072, 128)
    leaving = depart(vorticity, position, counts, vel)
    arrivals = [
        stepped(leaving[0], "gx", 1),
        stepped(leaving[1], "gx", -1),
        stepped(leaving[2], "gz", 1),
        stepped(leaving[3], "gz", -1),
    ]
    places, marks, kept = keep(owner_ids[:, 0], slot_ids, vorticity, position, counts)
    ship = route(places, marks, arrivals, kept)
    rows = exchange(ship.reshape(128, 25, 1, 128)).reshape(3200, 128)

    grads = gradient(vel, *arrivals)

    back, mesh = sample(rows, grads)
    back = exchange(back.reshape(128, 3, 4, 128)).reshape(1536, 128)
    mesh = deposit(rows, mesh)
    stretching = unpack(places, back)
    mesh = jnp.transpose(mesh.reshape(4, 16, 3, 16, 128), (0, 1, 3, 2, 4))
    return mesh, stretching


def solution(mesh):
    placed = (
        P(None, None, AXES),
        P(None, None, AXES),
        P(None, AXES),
        P(AXES, None),
        P(AXES),
        P("gx", None, "gz", None, None),
    )
    return jax.shard_map(
        on_device,
        mesh=mesh,
        in_specs=placed,
        out_specs=(P("gx", None, "gz", None, None), P(None, None, None, AXES)),
        check_vma=False,
    )
```
